32 devices in a mesh: pipe: 2 (over x), dp: 16 (over z, y, core).
Axes of the slice: x: 2, y: 2, z: 4, core: 2. Of those that a mesh axis runs over, the one named last changes fastest.
Arguments:
- tokens: bfloat16 [16384, 768], P('dp', 'pipe'), may hold values from -6 to 6
- out_cot: bfloat16 [16384, 768], P('dp', 'pipe'), may hold values from -6 to 6
- weight_cot: float32 [16384], P('dp'), may hold values from -6 to 6
- plan: int32 [32], P('dp'), may hold values 0 or 1
- lengths: int32 [32, 4], P('dp'), may hold values from 32 to 128
- q_weight: bfloat16 [2, 768, 768], P('pipe'), may hold values from -0.21875 to 0.21875
- k_weight: bfloat16 [2, 768, 768], P('pipe'), may hold values from -0.21875 to 0.21875
- v_weight: bfloat16 [2, 768, 768], P('pipe'), may hold values from -0.21875 to 0.21875
- o_weight: bfloat16 [2, 768, 768], P('pipe'), may hold values from -1.75 to 1.75
- q_bias: bfloat16 [2, 768], P('pipe'), may hold values from -1.75 to 1.75
- v_bias: bfloat16 [2, 768], P('pipe'), may hold values from -1.75 to 1.75
- o_bias: bfloat16 [2, 768], P('pipe'), may hold values from -1.75 to 1.75
- norm1_gain: bfloat16 [2, 768], P('pipe'), may hold values from 0.25 to 1.75
- norm1_bias: bfloat16 [2, 768], P('pipe'), may hold values from -1.75 to 1.75
- up_weight: bfloat16 [2, 768, 3072], P('pipe'), may hold values from -0.21875 to 0.21875
- up_bias: bfloat16 [2, 3072], P('pipe'), may hold values from -1.75 to 1.75
- down_weight: bfloat16 [2, 3072, 768], P('pipe'), may hold values from -0.109375 to 0.109375
- down_bias: bfloat16 [2, 768], P('pipe'), may hold values from -1.75 to 1.75
- norm2_gain: bfloat16 [2, 768], P('pipe'), may hold values from 0.25 to 1.75
- norm2_bias: bfloat16 [2, 768], P('pipe'), may hold values from -1.75 to 1.75
- head_weight: bfloat16 [768], replicated, may hold values from -0.21875 to 0.21875
- head_bias: float32 [1], replicated, may hold values from -1 to 1
Outputs:
- mixed: bfloat16 [16384, 768], P('dp', 'pipe')
- term_weights: float32 [16384], P('dp')
- tokens_grad: bfloat16 [16384, 768], P('dp', 'pipe')
- q_weight_grad: float32 [2, 768, 768], P('pipe', 'dp')
- k_weight_grad: float32 [2, 768, 768], P('pipe', 'dp')
- v_weight_grad: float32 [2, 768, 768], P('pipe', 'dp')
- o_weight_grad: float32 [2, 768, 768], P('pipe', 'dp')
- q_bias_grad: float32 [2, 768], P('pipe', 'dp')
- v_bias_grad: float32 [2, 768], P('pipe', 'dp')
- o_bias_grad: float32 [2, 768], P('pipe', 'dp')
- norm1_gain_grad: float32 [2, 768], P('pipe', 'dp')
- norm1_bias_grad: float32 [2, 768], P('pipe', 'dp')
- up_weight_grad: float32 [2, 768, 3072], P('pipe', 'dp')
- up_bias_grad: float32 [2, 3072], P('pipe', 'dp')
- down_weight_grad: float32 [2, 3072, 768], P('pipe', 'dp')
- down_bias_grad: float32 [2, 768], P('pipe', 'dp')
- norm2_gain_grad: float32 [2, 768], P('pipe', 'dp')
- norm2_bias_grad: float32 [2, 768], P('pipe', 'dp')
- head_weight_grad: float32 [768], P('dp')
- head_bias_grad: float32 [1], replicated
The draws below stay inside these ranges and needn't reach their ends.
Inputs may be any that keep to these rules, and one draw needn't show every extreme that they name: `plan`: 1 marks a slab holding one passage of 512 slots, 0 a slab of 4 passages of 128 slots. `lengths`: in a slab of short passages entry j is the number of real tokens of passage j, at its start; in a slab of one long passage the entries add up to its real tokens, at its start.
All inputs are finite; a program needn't handle non-finite values. No bound on the sum of `plan` on one device may be relied on, other than what follows from the above.
Results may differ from the reference program's by a relative error of at most 0.029.
Values may be sent and summed in bfloat16 or wider, within the bound.
No kernel may reach another device: no remote copies, remote signals or barrier semaphores. Data moves between devices by JAX's collectives and lax.ppermute only.
A program may use at most 256 MiB of HBM per device.

```python
import jax
import jax.numpy as jnp
from jax import lax

D = 768
HEADS = 12
HEAD = 64
FF = 3072
SHORT = 128
LONG = 512
SLOTS = 4
SLABS = 32
TOKENS = 16384


def plant(result, key, low, largest):
    longest = result.shape.index(max(result.shape))
    spots = []
    for shift in (0, 1):
        where = [jax.random.randint(jax.random.fold_in(key, axis), (), 0, length) for axis, length in enumerate(result.shape)]
        where[longest] = (where[longest] + shift) % result.shape[longest]
        spots.append(tuple(where))
    return result.at[spots[0]].set(low).at[spots[1]].set(largest)


def levels(key, extent, split, least, high):
    loudness, own = 1.0, jax.random.fold_in(key, 6)
    for axis_at, parts in split:
        heights = jnp.exp(jax.random.uniform(jax.random.fold_in(own, axis_at), (parts,), jnp.float32, least / len(split), high / len(split)))
        loudness = loudness * jnp.repeat(heights, extent[axis_at] // parts).reshape([-1 if axis == axis_at else 1 for axis in range(len(extent))])
    return loudness


def gaussian(own_key, extent, scale, bound, cuts=(), kind=jnp.bfloat16):
    factor_of = levels(own_key, extent, cuts, -0.22, 0.18) if cuts else 1.0
    array = jax.random.normal(own_key, extent, jnp.float32) * scale * factor_of
    return jnp.minimum(jnp.maximum(array, -bound), bound).astype(kind)


def setup_inputs(seed: int = 0) -> dict:
    key_of = jax.random.split(jax.random.key(seed), 23)
    return {
        "tokens": gaussian(key_of[0], (TOKENS, D), 1.0, 6.0, ((0, 16), (1, 2))),
        "out_cot": gaussian(key_of[1], (TOKENS, D), 1.0, 6.0, ((0, 16), (1, 2))),
        "weight_cot": gaussian(key_of[2], (TOKENS,), 1.0, 6.0, ((0, 16),), jnp.float32),
        "plan": plant((jax.random.randint(key_of[3], (SLABS,), 0, 3) < 1).astype(jnp.int32), jax.random.fold_in(key_of[3], 1), 0, 1),
        "lengths": plant(jax.random.randint(key_of[4], (SLABS, SLOTS), SHORT // 4, SHORT + 1), jax.random.fold_in(key_of[4], 1), SHORT // 4, SHORT).astype(jnp.int32),
        "q_weight": gaussian(key_of[5], (2, D, D), D ** -0.5, 0.21875, ((0, 2),)),
        "k_weight": gaussian(key_of[6], (2, D, D), D ** -0.5, 0.21875, ((0, 2),)),
        "v_weight": gaussian(key_of[7], (2, D, D), D ** -0.5, 0.21875, ((0, 2),)),
        "o_weight": gaussian(key_of[8], (2, D, D), (max(D // 64, 2)) ** -0.5, 1.75, ((0, 2),)),
        "q_bias": gaussian(key_of[9], (2, D), 0.3, 1.75, ((0, 2),)),
        "v_bias": gaussian(key_of[10], (2, D), 0.3, 1.75, ((0, 2),)),
        "o_bias": gaussian(key_of[11], (2, D), 0.3, 1.75, ((0, 2),)),
        "norm1_gain": jnp.clip(1.0 + 0.15 * jax.random.normal(key_of[12], (2, D), jnp.float32), 0.25, 1.75).astype(jnp.bfloat16),
        "norm1_bias": gaussian(key_of[13], (2, D), 0.3, 1.75, ((0, 2),)),
        "up_weight": gaussian(key_of[14], (2, D, FF), D ** -0.5, 0.21875, ((0, 2),)),
        "up_bias": gaussian(key_of[15], (2, FF), 0.3, 1.75, ((0, 2),)),
        "down_weight": gaussian(key_of[16], (2, FF, D), FF ** -0.5, 0.109375, ((0, 2),)),
        "down_bias": gaussian(key_of[17], (2, D), 0.3, 1.75, ((0, 2),)),
        "norm2_gain": jnp.clip(1.0 + 0.15 * jax.random.normal(key_of[18], (2, D), jnp.float32), 0.25, 1.75).astype(jnp.bfloat16),
        "norm2_bias": gaussian(key_of[19], (2, D), 0.3, 1.75, ((0, 2),)),
        "head_weight": gaussian(key_of[20], (D,), D ** -0.5, 0.21875),
        "head_bias": jnp.clip(jax.random.uniform(key_of[21], (1,), jnp.float32, -1.0, 1.0), -1.0, 1.0),
    }


@jax.custom_vjp
def low(v):
    return lax.optimization_barrier(v.astype(jnp.bfloat16)).astype(jnp.float32)

@jax.custom_vjp
def low_back(v):
    return v

def low_keep(v):
    return (low(v), None)

def low_pass(kept, grad):
    return (grad,)

def back_keep(v):
    return (v, None)

def back_low(kept, grad):
    return (low(grad),)
low.defvjp(low_keep, low_pass)
low_back.defvjp(back_keep, back_low)
EPSILON = 1e-06
MASKED = -1e+30
HIGHEST = lax.Precision.HIGHEST

def product(left_side, right_side):
    return jnp.dot(left_side, right_side, precision=HIGHEST)

def layer_norm(residual, gain_vec, offset):
    centre = residual - lax.optimization_barrier(jnp.mean(residual, axis=-1, keepdims=True))
    spread = lax.optimization_barrier(jnp.mean(centre * centre, axis=-1, keepdims=True))
    return centre * lax.rsqrt(spread + EPSILON) * gain_vec + offset

def soft_plus(argument):
    return jnp.maximum(argument, 0.0) + jnp.log1p(jnp.exp(-jnp.abs(argument)))

def slab_masks(slab_kind, slot_lengths):
    position = jnp.arange(LONG, dtype=jnp.int32)
    slot_index = position // SHORT
    within = position - slot_index * SHORT
    slot_ids = jnp.arange(LONG // SHORT, dtype=jnp.int32)
    own_length = lax.optimization_barrier(jnp.sum(jnp.where(slot_index[:, None] == slot_ids[None, :], slot_lengths[None, :], 0), axis=1))
    whole_length = jnp.sum(slot_lengths)
    segment = jnp.where(slab_kind == 1, 0, slot_index)
    valid_rows = jnp.where(slab_kind == 1, position < whole_length, within < own_length)
    allowed = (segment[:, None] == segment[None, :]) & valid_rows[None, :]
    return (allowed, valid_rows.astype(jnp.float32))

def block_layer(hidden, weights, allowed):
    q_weight, k_weight, v_weight, o_weight, q_bias, v_bias, o_bias, gain_one, offset_one, up_weight, up_bias, down_weight, down_bias, gain_two, offset_two = weights
    factor = HEAD ** (-0.5)
    hidden = low_back(hidden)
    queries = low(low_back(factor * (product(hidden, q_weight) + q_bias))).reshape(LONG, HEADS, HEAD)
    key_rows = low(low_back(product(hidden, k_weight))).reshape(LONG, HEADS, HEAD)
    values = low(low_back(product(hidden, v_weight) + v_bias)).reshape(LONG, HEADS, HEAD)
    scores = low_back(jnp.einsum('qhd,khd->hqk', queries, key_rows, precision=HIGHEST))
    scores = jnp.where(allowed[None], scores, MASKED)
    row_max = lax.optimization_barrier(jnp.max(scores, axis=2, keepdims=True))
    exponent = jnp.exp(scores - row_max)
    weights_low = low(exponent / lax.optimization_barrier(jnp.sum(exponent, axis=2, keepdims=True)))
    attended = jnp.einsum('hqk,khd->qhd', weights_low, values, precision=HIGHEST).reshape(LONG, D)
    attended = low(low_back(attended))
    branch = low_back(product(attended, o_weight) + o_bias)
    normed = layer_norm(hidden + branch, gain_one, offset_one)
    lifted = low_back(product(low(normed), up_weight) + up_bias)
    activated = low(jax.nn.gelu(lifted, approximate=False))
    dropped = low_back(product(activated, down_weight) + down_bias)
    return layer_norm(normed + dropped, gain_two, offset_two)

def reference(tokens, out_cot, weight_cot, plan, lengths, q_weight, k_weight, v_weight, o_weight, q_bias, v_bias, o_bias, norm1_gain, norm1_bias, up_weight, up_bias, down_weight, down_bias, norm2_gain, norm2_bias, head_weight, head_bias):
    stacked = (q_weight, k_weight, v_weight, o_weight, q_bias, v_bias, o_bias, norm1_gain, norm1_bias, up_weight, up_bias, down_weight, down_bias, norm2_gain, norm2_bias)
    first_layer = tuple((piece[0].astype(jnp.float32) for piece in stacked))
    second_layer = tuple((piece[1].astype(jnp.float32) for piece in stacked))
    inputs = tokens.astype(jnp.float32).reshape(SLABS, LONG, D)
    allowed_all, valid_all = jax.vmap(slab_masks)(plan, lengths)

    def forward(slabs, first_params, second_params, head_vec, head_shift):

        def one_slab(pieces):
            slab, slab_allowed, slab_valid = pieces
            passed = low(block_layer(slab, first_params, slab_allowed))
            output_rows = low(block_layer(passed, second_params, slab_allowed))
            pre_rows = product(output_rows, head_vec) + head_shift[0]
            return (output_rows, soft_plus(pre_rows) * slab_valid)
        return lax.map(jax.checkpoint(one_slab), (slabs, allowed_all, valid_all))
    (output_rows, term_rows), pull = jax.vjp(forward, inputs, first_layer, second_layer, head_weight.astype(jnp.float32), head_bias.astype(jnp.float32))
    cotangents = (out_cot.astype(jnp.float32).reshape(SLABS, LONG, D), weight_cot.reshape(SLABS, LONG))
    input_grad, first_grads, second_grads, head_vec_grad, head_shift_grad = pull(cotangents)
    grads = [jnp.stack([first_piece, second_piece]) for first_piece, second_piece in zip(first_grads, second_grads)]
    return (output_rows.reshape(TOKENS, D).astype(jnp.bfloat16), term_rows.reshape(TOKENS), input_grad.reshape(TOKENS, D).astype(jnp.bfloat16), grads[0], grads[1], grads[2], grads[3], grads[4], grads[5], grads[6], grads[7], grads[8], grads[9], grads[10], grads[11], grads[12], grads[13], grads[14], head_vec_grad, head_shift_grad)
```

```python
import functools
from types import SimpleNamespace

import jax
import jax.numpy as jnp
from jax import lax
from jax.experimental import pallas as pl
from jax.experimental.pallas import tpu as pltpu
from jax.sharding import PartitionSpec as P

HEADS = 12
HEAD = 64
PAIR = 2 * HEAD
PAIRS = HEADS // 2
SHORT = 128
LONG = 512
EPSILON = 1e-06
MASKED = -1e30
FACTOR = HEAD**-0.5
LOG2E = 1.4426950408889634
LN2 = 0.6931471805599453
BF = jnp.bfloat16
F32 = jnp.float32
VMEM_BYTES = 58 << 20


def product(dims, left_side, right_side):
    return lax.dot_general(left_side, right_side, (dims, ((), ())), preferred_element_type=F32)


nn = functools.partial(product, ((1,), (0,)))
nt = functools.partial(product, ((1,), (1,)))
tn = functools.partial(product, ((0,), (0,)))


def segment_limits(plan, lengths, slab, position):
    is_long = plan[slab] == 1
    parts = [lengths[slab, j] for j in range(LONG // SHORT)]
    slot = position // SHORT
    own = jnp.full(position.shape, parts[-1], jnp.int32)
    for j in range(len(parts) - 1):
        own = jnp.where(slot == j, parts[j], own)
    limit = jnp.where(is_long, sum(parts), own + slot * SHORT)
    return jnp.where(is_long, 0, slot), position < limit


def row_mean(rows_in):
    return jnp.mean(rows_in, axis=1, keepdims=True)


def column_sum(rows_in):
    return jnp.sum(rows_in.astype(F32), axis=0, keepdims=True)


def in_half(j):
    lane = lax.broadcasted_iota(jnp.int32, (LONG, PAIR), 1)
    return (lane < HEAD) if j == 0 else (lane >= HEAD)


def lane_block(index, width):
    start = index * width
    return pl.ds(start if isinstance(index, int) else pl.multiple_of(start, width), width)


class Copies:
    def __init__(self, sems):
        self.sems, self.used, self.named = sems, 0, {}

    def make(self, name, src, dst):
        copy = pltpu.make_async_copy(src, dst, self.sems.at[self.used])
        self.used += 1
        self.named[name] = copy
        return copy

    def start(self, name, src, dst):
        self.make(name, src, dst).start()

    def wait(self, *names):
        for name in names:
            self.named.pop(name).wait()

    def wait_all(self):
        self.wait(*list(self.named))


def call(name, body, scalars, local, far, outs, scratch, sems, cost, kept=None):
    kept = kept or {}
    names = list(scalars) + list(local) + list(far)
    arrays = list(scalars.values()) + list(local.values()) + list(far.values())
    specs = [pl.BlockSpec(memory_space=pltpu.SMEM)] * len(scalars)
    specs += [pl.BlockSpec(memory_space=pltpu.VMEM)] * len(local)
    specs += [pl.BlockSpec(memory_space=pl.ANY)] * (len(far) + len(kept))
    aliases = {}
    for key, array in kept.items():
        aliases[len(arrays)] = list(outs).index(key)
        arrays.append(array)
    skip = len(kept)

    def kernel(*refs):
        refs = list(refs)
        given, rest = refs[: len(names)], refs[len(names) + skip :]
        n = len(outs)
        body(
            SimpleNamespace(**dict(zip(names, given))),
            SimpleNamespace(**dict(zip(outs, rest[:n]))),
            SimpleNamespace(**dict(zip(scratch, rest[n : n + len(scratch)]))),
            Copies(rest[-1]),
        )

    made = pl.pallas_call(
        kernel,
        out_shape=[jax.ShapeDtypeStruct(d, k) for d, k in outs.values()],
        in_specs=specs,
        out_specs=[pl.BlockSpec(memory_space=pl.ANY)] * len(outs),
        scratch_shapes=[pltpu.VMEM(d, k) for d, k in scratch.values()]
        + [pltpu.SemaphoreType.DMA((sems,))],
        input_output_aliases=aliases,
        compiler_params=pltpu.CompilerParams(vmem_limit_bytes=VMEM_BYTES),
        cost_estimate=pl.CostEstimate(flops=cost, bytes_accessed=30_000_000, transcendentals=0),
        name=name,
    )(*arrays)
    return dict(zip(outs, made))


def active_slab(slab, count, run):
    pl.when((slab >= 0) & (slab < count))(run)


def forward_turn(turn, count, section, plan, lengths, own, other, recv, weights, vectors, kept):
    wide, deep = weights["wq"].shape[1], weights["up"].shape[2]
    half = own.shape[1]
    rows = (LONG, wide)
    stack = {
        "h": (rows, BF), "q": (rows, BF), "k": (rows, BF), "v": (rows, BF),
        "p": ((HEADS, LONG, LONG), BF), "att": (rows, BF), "full": (rows, F32),
        "rinv": (rows, F32), "xh1": (rows, BF), "nl": (rows, BF), "act": ((LONG, deep), BF),
        "dg": ((LONG, deep), BF), "xh2": (rows, BF), "st": ((LONG, 128), F32), "out": (rows, BF),
    }
    outs = {n: ((count,) + d, k) for n, (d, k) in stack.items()}
    outs["sent"] = (rows, BF)
    scratch = dict(stack)
    scratch.update({n: (w.shape[1:], BF) for n, w in weights.items()})
    scratch.update({
        "normed": (rows, F32), "acc": (rows, F32), "qfeat": ((LONG, PAIR), BF),
        "kfeat": ((LONG, PAIR), BF),
    })
    far = dict(weights, own=own, other=other)
    if recv is not None:
        far["recv"] = recv
    chunk = wide
    chunks = deep // chunk

    def body(i, o, s, copies):
        slab = turn - i.section[0]
        first = i.section[0] == 0

        def run():
            for n in ("wq", "wk", "wv"):
                copies.start(n, getattr(i, n).at[0], getattr(s, n))
            mine = pl.ds(pl.multiple_of(slab * LONG, LONG), LONG)
            left = copies.make("left", i.own.at[mine], s.h.at[:, pl.ds(0, half)])
            right = copies.make("right", i.other, s.h.at[:, pl.ds(half, half)])

            def tokens_in():
                left.start()
                right.start()
                left.wait()
                right.wait()

            if recv is None:
                tokens_in()
            else:
                whole = copies.make("whole", i.recv, s.h)

                def recv_in():
                    whole.start()
                    whole.wait()

                pl.when(first)(tokens_in)
                pl.when(jnp.logical_not(first))(recv_in)
            copies.named.pop("left")
            copies.named.pop("right")
            copies.named.pop("whole", None)
            copies.start("wo", i.wo.at[0], s.wo)
            for c in range(chunks):
                cols = lane_block(c, chunk)
                copies.start(f"up{c}", i.up.at[0, :, cols], s.up.at[:, cols])
                copies.start(f"down{c}", i.down.at[0, cols, :], s.down.at[cols, :])

            def store(name):
                copies.start("o" + name, getattr(s, name), getattr(o, name).at[slab])

            lane = lax.broadcasted_iota(jnp.int32, (LONG, PAIR), 1) % HEAD
            at = lax.broadcasted_iota(jnp.int32, (LONG, PAIR), 0)
            segment, valid = segment_limits(i.plan, i.lengths, slab, at)
            s.qfeat[...] = jnp.where(segment == lane, 1.0, 0.0).astype(BF)
            closed = (lane < LONG // SHORT) & ((segment != lane) | jnp.logical_not(valid))
            s.kfeat[...] = jnp.where(closed, MASKED, 0.0).astype(BF)
            hidden = s.h[...]
            store("h")
            copies.wait("wq")
            queries = nn(hidden, s.wq[...]) + i.qb[...].astype(F32)
            s.q[...] = (queries * (FACTOR * LOG2E)).astype(BF)
            store("q")
            copies.wait("wk")
            s.k[...] = nn(hidden, s.wk[...]).astype(BF)
            store("k")
            copies.wait("wv")
            s.v[...] = (nn(hidden, s.wv[...]) + i.vb[...].astype(F32)).astype(BF)
            store("v")
            base = copies.used
            copies.used += PAIRS

            def probs_out(pair):
                two = pl.ds(2 * pair, 2)
                return pltpu.make_async_copy(
                    s.p.at[two], o.p.at[slab, two], copies.sems.at[base + pair]
                )

            def pair_step(pair, carry):
                cols = lane_block(pair, PAIR)
                qp, kp, vp = s.q[:, cols], s.k[:, cols], s.v[:, cols]
                sides = []
                for j in range(2):
                    here = in_half(j)
                    scores = nt(
                        jnp.where(here, qp, s.qfeat[...]), jnp.where(here, kp, s.kfeat[...])
                    )
                    top = jnp.max(scores, axis=1, keepdims=True)
                    raised = jnp.exp2(scores - top).astype(BF)
                    s.p[2 * pair + j] = raised
                    sides.append(nn(raised, jnp.where(here, vp, jnp.ones_like(vp))))
                low = in_half(0)
                rinv = 1.0 / pltpu.roll(jnp.where(low, sides[1], sides[0]), HEAD, 1)
                mix = jnp.where(low, sides[0], sides[1]) * rinv
                s.full[:, cols] = mix
                s.rinv[:, cols] = rinv
                s.att[:, cols] = mix.astype(BF)
                probs_out(pair).start()
                return carry

            lax.fori_loop(0, PAIRS, pair_step, 0, unroll=2)
            for n in ("att", "full", "rinv"):
                store(n)
            copies.wait("wo")
            res = hidden.astype(F32) + (nn(s.att[...], s.wo[...]) + i.ob[...].astype(F32))
            centre = res - row_mean(res)
            rstd1 = lax.rsqrt(row_mean(centre * centre) + EPSILON)
            xhat = centre * rstd1
            normed = xhat * i.g1[...].astype(F32) + i.b1[...].astype(F32)
            s.xh1[...] = xhat.astype(BF)
            s.nl[...] = normed.astype(BF)
            s.normed[...] = normed
            store("xh1")
            store("nl")
            for c in range(chunks):
                cols = lane_block(c, chunk)
                copies.wait(f"up{c}")
                lifted = nn(s.nl[...], s.up[:, cols]) + i.upb[:, cols].astype(F32)
                cdf = 0.5 + 0.5 * lax.erf(lifted * 0.7071067811865476)
                act = (lifted * cdf).astype(BF)
                dens = jnp.exp2(lifted * lifted * (-0.5 * LOG2E)) * 0.3989422804014327
                s.act[:, cols] = act
                s.dg[:, cols] = (cdf + lifted * dens).astype(BF)
                copies.wait(f"down{c}")
                part = nn(act, s.down[cols, :])
                s.acc[...] = part if c == 0 else s.acc[...] + part
                copies.start(f"act{c}", s.act.at[:, cols], o.act.at[slab, :, cols])
                copies.start(f"dg{c}", s.dg.at[:, cols], o.dg.at[slab, :, cols])
            res = s.normed[...] + s.acc[...] + i.downb[...].astype(F32)
            centre = res - row_mean(res)
            rstd2 = lax.rsqrt(row_mean(centre * centre) + EPSILON)
            xhat = centre * rstd2
            s.out[...] = (xhat * i.g2[...].astype(F32) + i.b2[...].astype(F32)).astype(BF)
            copies.start("sent", s.out, o.sent)
            store("out")
            s.xh2[...] = xhat.astype(BF)
            store("xh2")
            side = lax.broadcasted_iota(jnp.int32, (LONG, 128), 1)
            s.st[...] = jnp.where(side < 64, rstd1, rstd2)
            store("st")
            for pair in range(PAIRS):
                probs_out(pair).wait()
            copies.wait_all()

        active_slab(slab, count, run)

    made = call(
        "forward_layer", body, dict(section=section, plan=plan, lengths=lengths), vectors, far,
        outs, scratch, 64, 16_000_000_000, kept,
    )
    sent = made.pop("sent")
    return made, sent


def norm_back(grad, xhat, rstd, gain):
    scaled = grad * gain
    return rstd * (scaled - row_mean(scaled) - xhat * row_mean(scaled * xhat))


def backward_turn(turn, count, phases, scalars, vectors, cots, weights, kept, passed, made):
    do_norm, do_feed, do_attn = (n in phases for n in ("norm", "feed", "attn"))
    wide, deep = kept["h"].shape[2], kept["act"].shape[2]
    rows = (LONG, wide)
    half = wide // 2
    chunk = wide
    chunks = deep // chunk
    stacks, loose = {}, {}
    uses, needs, links = [], [], []
    if do_norm:
        stacks.update(ddown=(rows, BF), vec0=((8, wide), F32), term=((8, LONG), F32))
        uses += ["out", "xh2", "st"]
    if do_feed:
        stacks.update(dlift=((LONG, deep), BF), dbranch=(rows, BF), vec1=((8, wide), F32))
        uses += ["dg", "xh1"] + ([] if do_norm else ["st"])
        needs += ["down", "up"]
    if do_attn:
        stacks.update(dqkv=((LONG, 3 * wide), BF), vec2=((8, wide), F32), dh=(rows, BF))
        uses += ["full", "rinv", "q", "k", "v", "p"]
        needs += ["wo", "wq", "wk", "wv"]
        loose.update(sent=(rows, BF))
    if do_norm and not do_feed:
        loose.update(dr2=(rows, F32))
    if do_feed and not do_attn:
        loose.update(dr1=(rows, F32))
    if do_feed and not do_norm:
        links += ["dr2", "ddown"]
    if do_attn and not do_feed:
        links += ["dr1", "dbranch"]
    far = {"r_" + n: kept[n] for n in uses}
    far.update({n: weights[n] for n in needs})
    far.update({"l_" + n: passed[n] for n in links})
    if do_norm:
        far.update({n: a for n, a in cots.items() if a is not None})
    outs = {n: ((count,) + d, k) for n, (d, k) in stacks.items()}
    outs.update(loose)
    scratch = {n: (kept[n].shape[1:], kept[n].dtype) for n in uses}
    scratch.update({n: (weights[n].shape[1:], BF) for n in needs})
    scratch.update(stacks)
    scratch.update(dr2=(rows, F32), dr1=(rows, F32))
    if do_norm:
        scratch.update(cot=(rows, BF))
    if do_feed:
        scratch.update(acc=(rows, F32), ddown=(rows, BF))
    if do_attn:
        scratch.update(datt=(rows, BF), dbranch=(rows, BF))

    def body(i, o, s, copies):
        slab = count - turn - i.section[0]
        first = i.section[0] == 0

        def get(name):
            copies.start("r_" + name, getattr(i, "r_" + name).at[slab], getattr(s, name))

        def get_weight(name):
            copies.start(name, getattr(i, name).at[0], getattr(s, name))

        def put(name):
            copies.start("o" + name, getattr(s, name), getattr(o, name).at[slab])

        def norm_loads():
            for n in ("out", "xh2", "st"):
                get(n)
            mine = pl.ds(pl.multiple_of(slab * LONG, LONG), LONG)
            left = copies.make("left", i.other, s.cot.at[:, pl.ds(0, half)])
            right = copies.make("right", i.own.at[mine], s.cot.at[:, pl.ds(half, half)])

            def own_in():
                left.start()
                right.start()

            def own_wait():
                left.wait()
                right.wait()

            if not hasattr(i, "recv"):
                own_in()
                return own_wait
            whole = copies.make("whole", i.recv, s.cot)
            pl.when(first)(whole.start)
            pl.when(jnp.logical_not(first))(own_in)

            def either_wait():
                pl.when(first)(whole.wait)
                pl.when(jnp.logical_not(first))(own_wait)

            return either_wait

        def feed_loads():
            for c in range(chunks):
                cols = lane_block(c, chunk)
                copies.start(f"down{c}", i.down.at[0, cols, :], s.down.at[cols, :])
                copies.start(f"dg{c}", i.r_dg.at[slab, :, cols], s.dg.at[:, cols])
                copies.start(f"up{c}", i.up.at[0, :, cols], s.up.at[:, cols])
            get("xh1")

        def attn_loads():
            get_weight("wo")
            for n in ("rinv", "full", "v", "k", "q"):
                get(n)
            for pair in range(PAIRS):
                two = pl.ds(2 * pair, 2)
                copies.start(f"p{pair}", i.r_p.at[slab, two], s.p.at[two])
            for n in ("wq", "wk", "wv"):
                get_weight(n)

        def norm_phase(wait_cot):
            position = lax.broadcasted_iota(jnp.int32, (LONG, 1), 0)
            valid = segment_limits(i.plan, i.lengths, slab, position)[1]
            valid = jnp.where(valid, 1.0, 0.0)
            cot_row = jnp.broadcast_to(i.weight_cot[slab], (8, LONG))
            cot_column = jnp.transpose(cot_row)[:, :1]
            cot_column = jnp.where(first, 0.0, cot_column * valid)
            copies.wait("r_out")
            mixed = s.out[...].astype(F32)
            head = i.head_weight[...].astype(F32)
            pre = jnp.sum(mixed * head, axis=1, keepdims=True) + i.head_bias[0]
            term = jnp.maximum(pre, 0.0) + jnp.log1p(jnp.exp(-jnp.abs(pre)))
            s.term[...] = jnp.transpose(jnp.broadcast_to(term * valid, (LONG, 128)))[:8]
            put("term")
            g_pre = cot_column / (1.0 + jnp.exp(-pre))
            wait_cot()
            grad = s.cot[...].astype(F32) + g_pre * head
            s.vec0[3:4, :] = column_sum(g_pre * mixed)
            s.vec0[4:5, :] = jnp.broadcast_to(column_sum(g_pre), (1, wide))
            copies.wait("r_xh2", "r_st")
            xhat = s.xh2[...].astype(F32)
            s.vec0[0:1, :] = column_sum(grad * xhat)
            s.vec0[1:2, :] = column_sum(grad)
            dr2 = norm_back(grad, xhat, s.st[:, 64:65], i.g2[...].astype(F32))
            s.dr2[...] = dr2
            s.ddown[...] = dr2.astype(BF)
            put("ddown")
            s.vec0[2:3, :] = column_sum(s.ddown[...])
            put("vec0")

        def feed_phase():
            for c in range(chunks):
                cols = lane_block(c, chunk)
                copies.wait(f"down{c}", f"dg{c}")
                dact = nt(s.ddown[...], s.down[cols, :])
                dlift = (dact * s.dg[:, cols].astype(F32)).astype(BF)
                s.dlift[:, cols] = dlift
                s.vec1[3 + c : 4 + c, :] = column_sum(dlift)
                copies.wait(f"up{c}")
                part = nt(dlift, s.up[:, cols])
                s.acc[...] = part if c == 0 else s.acc[...] + part
                copies.start(f"dlift{c}", s.dlift.at[:, cols], o.dlift.at[slab, :, cols])
            copies.wait("r_xh1")
            dnormed = s.dr2[...] + s.acc[...]
            xhat = s.xh1[...].astype(F32)
            s.vec1[0:1, :] = column_sum(dnormed * xhat)
            s.vec1[1:2, :] = column_sum(dnormed)
            dr1 = norm_back(dnormed, xhat, s.st[:, 0:1], i.g1[...].astype(F32))
            s.dr1[...] = dr1
            s.dbranch[...] = dr1.astype(BF)
            put("dbranch")
            s.vec1[2:3, :] = column_sum(s.dbranch[...])
            put("vec1")

        def attn_phase():
            copies.wait("wo")
            s.datt[...] = nt(s.dbranch[...], s.wo[...]).astype(BF)
            copies.wait("r_rinv", "r_full", "r_v", "r_k", "r_q")
            waits = [copies.named.pop(f"p{pair}") for pair in range(PAIRS)]
            for pair in range(PAIRS):
                waits[pair].wait()

            def pair_step(pair, carry):
                cols = lane_block(pair, PAIR)
                qp, kp, vp = s.q[:, cols], s.k[:, cols], s.v[:, cols]
                scaled = (s.datt[:, cols].astype(F32) * s.rinv[:, cols]).astype(BF)
                joint = scaled.astype(F32) * s.full[:, cols]
                parts = []
                for j in range(2):
                    here = in_half(j)
                    own = jnp.where(here, scaled, jnp.zeros_like(scaled))
                    delta = jnp.sum(jnp.where(here, joint, 0.0), axis=1, keepdims=True)
                    raised = s.p[2 * pair + j]
                    dscores = (raised.astype(F32) * (nt(own, vp) - delta)).astype(BF)
                    parts.append((nn(dscores, kp), tn(dscores, qp), tn(raised, scaled)))
                low = in_half(0)
                dq, dk, dv = (jnp.where(low, a, b) for a, b in zip(*parts))
                s.dqkv[:, cols] = (dq.astype(BF).astype(F32) * FACTOR).astype(BF)
                s.dqkv[:, lane_block(pair + PAIRS, PAIR)] = (dk * LN2).astype(BF)
                s.dqkv[:, lane_block(pair + 2 * PAIRS, PAIR)] = dv.astype(BF)
                return carry

            lax.fori_loop(0, PAIRS, pair_step, 0, unroll=2)
            put("dqkv")
            total = s.dr1[...]
            for n, name in enumerate(("wq", "wk", "wv")):
                copies.wait(name)
                total = total + nt(s.dqkv[:, lane_block(n, wide)], getattr(s, name)[...])
            s.dh[...] = total.astype(BF)
            copies.start("sent", s.dh, o.sent)
            put("dh")
            s.vec2[0:1, :] = column_sum(s.dqkv[:, lane_block(0, wide)])
            s.vec2[1:2, :] = column_sum(s.dqkv[:, lane_block(2, wide)])
            put("vec2")

        def run():
            wait_cot = norm_loads() if do_norm else None
            if do_feed and not do_norm:
                get("st")
            for n in links:
                far_ref = getattr(i, "l_" + n)
                copies.start(
                    "l_" + n, far_ref if n in ("dr1", "dr2") else far_ref.at[slab], getattr(s, n)
                )
            if do_feed:
                feed_loads()
            elif do_attn:
                attn_loads()
            if do_norm:
                norm_phase(wait_cot)
            if do_feed and do_attn:
                attn_loads()
            copies.wait(*["l_" + n for n in links])
            if do_feed:
                if not do_norm:
                    copies.wait("r_st")
                feed_phase()
            if do_attn:
                attn_phase()
            for n in loose:
                if n != "sent":
                    copies.start("o" + n, getattr(s, n), getattr(o, n))
            for n in ("left", "right", "whole"):
                copies.named.pop(n, None)
            copies.wait_all()

        active_slab(slab, count, run)

    local = {}
    if do_norm:
        local.update({n: vectors[n] for n in ("head_weight", "weight_cot", "g2")})
    if do_feed:
        local.update(g1=vectors["g1"])
    result = call(
        "backward_" + "_".join(phases), body, scalars, local, far, outs, scratch, 72,
        6_000_000_000 * len(phases), {n: made[n] for n in stacks} if made else None,
    )
    return {n: result[n] for n in stacks}, {n: result[n] for n in loose}


def weight_grad(left_rows, right_rows):
    left = left_rows.reshape(-1, left_rows.shape[-1])
    right = right_rows.reshape(-1, right_rows.shape[-1])
    return tn(left, right).astype(BF)


def pick(array_in, index, axis):
    return lax.dynamic_index_in_dim(array_in, index, axis, keepdims=False)


def cut(array_in, start, size):
    return lax.dynamic_slice_in_dim(array_in, start, size, 0)


def added(*pieces):
    total = pieces[0].astype(F32)
    for piece in pieces[1:]:
        total = total + piece.astype(F32)
    return total


def routed(block, pairs):
    return lax.ppermute(block, "dp", pairs)


def swap_bit(block, bit):
    return routed(block, [(i, i ^ bit) for i in range(lax.axis_size("dp"))])


def line_sum(blocks, place):
    row = range(4)
    inward = cut(blocks, jnp.where(place == 0, 1, 0), 3)
    ends = routed(inward, [(j, j + 4) for j in row] + [(j + 12, j + 8) for j in row])
    lower = place <= 1
    across = added(
        cut(blocks, jnp.where(lower, 2, 0), 2), cut(ends, jnp.where(lower, 1, 0), 2)
    ).astype(BF)
    middle = routed(across, [(j + 4, j + 8) for j in row] + [(j + 8, j + 4) for j in row])
    outward = added(
        pick(blocks, jnp.where(lower, 0, 3), 0), pick(middle, jnp.where(lower, 0, 1), 0)
    ).astype(BF)
    last = routed(outward, [(j + 4, j) for j in row] + [(j + 8, j + 12) for j in row])
    return (
        pick(blocks, place, 0),
        pick(ends, jnp.where(lower, 0, 2), 0),
        pick(middle, jnp.where(lower, 1, 0), 0),
        last,
    )


def reduce_shards(grad, extra=None, line_first=False):
    count = lax.axis_size("dp")
    me = lax.axis_index("dp")
    share = grad.shape[0] // count
    if count != 16:
        whole = lax.psum_scatter(grad.astype(F32), "dp", scatter_dimension=0, tiled=True)
        if extra is None:
            return whole
        return whole, lax.psum_scatter(extra, "dp", scatter_dimension=0, tiled=True)[0]
    core, side, place = me % 2, (me // 2) % 2, me // 4
    parts = grad.reshape(4, 2, 2, share, grad.shape[1])
    if extra is not None:
        lanes = -(-extra.shape[1] // share)
        lanes = -(-lanes // 128) * 128
        tail = jnp.pad(extra, ((0, 0), (0, share * lanes - extra.shape[1])))
        tail = tail.reshape(4, 2, 2, share, lanes)
        chosen = lambda which: jnp.concatenate(
            [pick(parts, which, 2), pick(tail, which, 2).astype(BF)], axis=-1
        )
    else:
        chosen = lambda which: pick(parts, which, 2)
    got = swap_bit(chosen(1 - core), 1)
    mine = chosen(core)
    if line_first:
        pairs = added(*line_sum(added(mine, got).astype(BF), place))
        back = swap_bit(pick(pairs, 1 - side, 0).astype(BF), 2)
        total = added(pick(pairs, side, 0), back)
    else:
        send = added(pick(mine, 1 - side, 1), pick(got, 1 - side, 1)).astype(BF)
        keep = added(pick(mine, side, 1), pick(got, side, 1)).astype(BF)
        total = added(*line_sum(added(keep, swap_bit(send, 2)).astype(BF), place))
    if extra is None:
        return total
    wide = grad.shape[1]
    return total[:, :wide], total[:, wide:].reshape(-1)[: extra.shape[1]]


def body(
    tokens,
    out_cot,
    weight_cot,
    plan,
    lengths,
    q_weight,
    k_weight,
    v_weight,
    o_weight,
    q_bias,
    v_bias,
    o_bias,
    norm1_gain,
    norm1_bias,
    up_weight,
    up_bias,
    down_weight,
    down_bias,
    norm2_gain,
    norm2_bias,
    head_weight,
    head_bias,
):
    my_section = lax.axis_index("pipe")
    is_first = my_section == 0
    section = my_section.astype(jnp.int32)[None]
    row_count, half = tokens.shape
    wide, deep = up_weight.shape[1:]
    count = row_count // LONG
    dp_count = lax.axis_size("dp")
    share = wide // dp_count
    to_both, to_next, to_back = [(0, 1), (1, 0)], [(0, 1)], [(1, 0)]
    partner = [
        lax.ppermute(
            jnp.where(is_first, out_cot[j * LONG : (j + 1) * LONG], tokens[j * LONG : (j + 1) * LONG]),
            "pipe",
            to_both,
        )
        for j in range(count)
    ]
    weights = dict(
        wq=q_weight, wk=k_weight, wv=v_weight, wo=o_weight, up=up_weight, down=down_weight
    )
    vectors = dict(
        qb=q_bias, vb=v_bias, ob=o_bias, g1=norm1_gain, b1=norm1_bias, upb=up_bias,
        downb=down_bias, g2=norm2_gain, b2=norm2_bias,
    )
    kept = recv = None
    for turn in range(count + 1):
        kept, sent = forward_turn(
            turn, count, section, plan, lengths, tokens, partner[min(turn, count - 1)], recv,
            weights, vectors, kept,
        )
        if turn < count:
            recv = lax.ppermute(sent, "pipe", to_next)
    scalars = dict(section=section, plan=plan, lengths=lengths, head_bias=head_bias)
    vectors = dict(
        g1=norm1_gain, g2=norm2_gain, head_weight=head_weight[None],
        weight_cot=weight_cot.reshape(count, 1, LONG),
    )
    made = recv = None
    for turn in range(count):
        cots = dict(own=out_cot, other=partner[count - 1 - turn], recv=recv)
        made, loose = backward_turn(
            turn, count, ("norm", "feed", "attn"), scalars, vectors, cots, weights, kept, {}, made
        )
        recv = lax.ppermute(loose["sent"], "pipe", to_back)
    cots = dict(own=out_cot, other=partner[0], recv=recv)
    step, loose = backward_turn(
        count, count, ("norm",), scalars, vectors, cots, weights, kept, {}, made
    )
    made = dict(made, **step)
    down_grad = reduce_shards(weight_grad(kept["act"], made["ddown"]))
    step, loose = backward_turn(
        count, count, ("feed",), scalars, vectors, cots, weights, kept,
        dict(loose, ddown=made["ddown"]), made,
    )
    made = dict(made, **step)
    up_grad = reduce_shards(weight_grad(kept["nl"], made["dlift"]))
    o_grad = reduce_shards(weight_grad(kept["att"], made["dbranch"]), line_first=True)
    step, loose = backward_turn(
        count, count, ("attn",), scalars, vectors, cots, weights, kept,
        dict(loose, dbranch=made["dbranch"]), made,
    )
    made = dict(made, **step)
    head_sums = jnp.sum(made["vec0"][:, 3:5], axis=0)
    term = made["term"][:, 0].reshape(row_count)
    early = jnp.concatenate([term, head_sums[0], head_sums[1, :1]])
    early_got = lax.ppermute(early, "pipe", to_back)
    early = jnp.where(is_first, early_got, early)
    sums0, sums1, sums2 = (jnp.sum(made[n], axis=0) for n in ("vec0", "vec1", "vec2"))
    lines = jnp.concatenate(
        [sums2[:2], sums1[2:3], sums1[:2], sums0[2:3], sums0[:2], early[None, row_count:-1]]
    )
    flat = jnp.concatenate(
        [
            lines.reshape(9, dp_count, share).transpose(1, 0, 2).reshape(dp_count, -1),
            sums1[3 : 3 + deep // wide].reshape(dp_count, -1),
            jnp.broadcast_to(early[None, -1:], (dp_count, 1)),
        ],
        axis=1,
    )
    qkv_grad, flat = reduce_shards(weight_grad(kept["h"], made["dqkv"]), extra=flat)
    at = lambda j: flat[j * share : (j + 1) * share]
    out_rows = kept["out"].reshape(row_count, wide)
    grad_rows = made["dh"].reshape(row_count, wide)
    mixed_got = lax.ppermute(out_rows[:, :half], "pipe", to_back)
    token_got = lax.ppermute(grad_rows[:, half:], "pipe", to_next)
    mixed_out = jnp.where(is_first, mixed_got, out_rows[:, half:])
    tokens_grad = jnp.where(is_first, grad_rows[:, :half], token_got)
    return (
        mixed_out,
        early[:row_count],
        tokens_grad,
        qkv_grad[None, :, :wide],
        qkv_grad[None, :, wide : 2 * wide],
        qkv_grad[None, :, 2 * wide :],
        o_grad[None],
        at(0)[None],
        at(1)[None],
        at(2)[None],
        at(3)[None],
        at(4)[None],
        up_grad[None],
        flat[None, 9 * share : 9 * share + deep // dp_count],
        down_grad[None],
        at(5)[None],
        at(6)[None],
        at(7)[None],
        at(8),
        flat[-1:],
    )


def solution(mesh):
    rows, stack, flat = P("dp", "pipe"), P("pipe", None, None), P("pipe", None)
    in_specs = (
        (rows, rows, P("dp"), P("dp"), P("dp", None))
        + (stack,) * 4
        + (flat,) * 5
        + (stack, flat, stack, flat, flat, flat, P(), P())
    )
    shard, line = P("pipe", "dp", None), P("pipe", "dp")
    out_specs = (
        (rows, P("dp"), rows)
        + (shard,) * 4
        + (line,) * 5
        + (shard, line, shard, line, line, line, P("dp"), P())
    )
    return jax.shard_map(body, mesh=mesh, in_specs=in_specs, out_specs=out_specs, check_vma=False)
```

```python
import functools
from types import SimpleNamespace

import jax
import jax.numpy as jnp
from jax import lax
from jax.experimental import pallas as pl
from jax.experimental.pallas import tpu as pltpu
from jax.sharding import PartitionSpec as P

HEADS = 12
HEAD = 64
PAIR = 2 * HEAD
PAIRS = HEADS // 2
SHORT = 128
LONG = 512
EPSILON = 1e-06
MASKED = -1e30
FACTOR = HEAD**-0.5
LOG2E = 1.4426950408889634
LN2 = 0.6931471805599453
BF = jnp.bfloat16
F32 = jnp.float32
VMEM_BYTES = 58 << 20


def product(dims, left_side, right_side):
    return lax.dot_general(left_side, right_side, (dims, ((), ())), preferred_element_type=F32)


nn = functools.partial(product, ((1,), (0,)))
nt = functools.partial(product, ((1,), (1,)))
tn = functools.partial(product, ((0,), (0,)))


def segment_limits(plan, lengths, slab, position):
    is_long = plan[slab] == 1
    parts = [lengths[slab, j] for j in range(LONG // SHORT)]
    slot = position // SHORT
    own = jnp.full(position.shape, parts[-1], jnp.int32)
    for j in range(len(parts) - 1):
        own = jnp.where(slot == j, parts[j], own)
    limit = jnp.where(is_long, sum(parts), own + slot * SHORT)
    return jnp.where(is_long, 0, slot), position < limit


def row_mean(rows_in):
    return jnp.mean(rows_in, axis=1, keepdims=True)


def column_sum(rows_in):
    return jnp.sum(rows_in.astype(F32), axis=0, keepdims=True)


def in_half(j):
    lane = lax.broadcasted_iota(jnp.int32, (LONG, PAIR), 1)
    return (lane < HEAD) if j == 0 else (lane >= HEAD)


def lane_block(index, width):
    start = index * width
    return pl.ds(start if isinstance(index, int) else pl.multiple_of(start, width), width)


class Copies:
    def __init__(self, sems):
        self.sems, self.used, self.named = sems, 0, {}

    def make(self, name, src, dst):
        copy = pltpu.make_async_copy(src, dst, self.sems.at[self.used])
        self.used += 1
        self.named[name] = copy
        return copy

    def start(self, name, src, dst):
        self.make(name, src, dst).start()

    def wait(self, *names):
        for name in names:
            self.named.pop(name).wait()

    def wait_all(self):
        self.wait(*list(self.named))


def call(name, body, scalars, local, far, outs, scratch, sems, cost, kept=None):
    kept = kept or {}
    names = list(scalars) + list(local) + list(far)
    arrays = list(scalars.values()) + list(local.values()) + list(far.values())
    specs = [pl.BlockSpec(memory_space=pltpu.SMEM)] * len(scalars)
    specs += [pl.BlockSpec(memory_space=pltpu.VMEM)] * len(local)
    specs += [pl.BlockSpec(memory_space=pl.ANY)] * (len(far) + len(kept))
    aliases = {}
    for key, array in kept.items():
        aliases[len(arrays)] = list(outs).index(key)
        arrays.append(array)
    skip = len(kept)

    def kernel(*refs):
        refs = list(refs)
        given, rest = refs[: len(names)], refs[len(names) + skip :]
        n = len(outs)
        body(
            SimpleNamespace(**dict(zip(names, given))),
            SimpleNamespace(**dict(zip(outs, rest[:n]))),
            SimpleNamespace(**dict(zip(scratch, rest[n : n + len(scratch)]))),
            Copies(rest[-1]),
        )

    made = pl.pallas_call(
        kernel,
        out_shape=[jax.ShapeDtypeStruct(d, k) for d, k in outs.values()],
        in_specs=specs,
        out_specs=[pl.BlockSpec(memory_space=pl.ANY)] * len(outs),
        scratch_shapes=[pltpu.VMEM(d, k) for d, k in scratch.values()]
        + [pltpu.SemaphoreType.DMA((sems,))],
        input_output_aliases=aliases,
        compiler_params=pltpu.CompilerParams(vmem_limit_bytes=VMEM_BYTES),
        cost_estimate=pl.CostEstimate(flops=cost, bytes_accessed=30_000_000, transcendentals=0),
        name=name,
    )(*arrays)
    return dict(zip(outs, made))


def forward_slab(
    role, slab, count, section, plan, lengths, own, other, recv, weights, vectors, kept, after
):
    wide, deep = weights["wq"].shape[1], weights["up"].shape[2]
    half = wide // 2
    rows = (LONG, wide)
    stack = {
        "h": (rows, BF), "q": (rows, BF), "k": (rows, BF), "v": (rows, BF),
        "p": ((HEADS, LONG, LONG), BF), "att": (rows, BF), "full": (rows, F32),
        "rinv": (rows, F32), "xh1": (rows, BF), "nl": (rows, BF), "act": ((LONG, deep), BF),
        "dg": ((LONG, deep), BF), "xh2": (rows, BF), "st": ((LONG, 128), F32), "out": (rows, BF),
    }
    outs = {n: ((count,) + d, k) for n, (d, k) in stack.items()}
    outs["sent"] = (rows, BF)
    scratch = dict(stack)
    scratch.update({n: (w.shape[1:], BF) for n, w in weights.items()})
    scratch.update({
        "normed": (rows, F32), "acc": (rows, F32), "qfeat": ((LONG, PAIR), BF),
        "kfeat": ((LONG, PAIR), BF),
    })
    far = dict(weights)
    far.update(dict(own=own, other=other) if role == 0 else dict(recv=recv))
    far.update({f"after{n}": array for n, array in enumerate(after)})
    chunk = wide
    chunks = deep // chunk

    def body(i, o, s, copies):
        def run():
            if role == 0:
                mine = pl.ds(slab * LONG, LONG)
                copies.start("left", i.own.at[mine], s.h.at[:, pl.ds(0, half)])
                copies.start("right", i.other, s.h.at[:, pl.ds(half, half)])
            else:
                copies.start("left", i.recv, s.h)
            for n in ("wq", "wk", "wv"):
                copies.start(n, getattr(i, n).at[0], getattr(s, n))
            copies.start("wo", i.wo.at[0], s.wo)
            for c in range(chunks):
                cols = lane_block(c, chunk)
                copies.start(f"up{c}", i.up.at[0, :, cols], s.up.at[:, cols])
                copies.start(f"down{c}", i.down.at[0, cols, :], s.down.at[cols, :])

            def store(name):
                copies.start("o" + name, getattr(s, name), getattr(o, name).at[slab])

            lane = lax.broadcasted_iota(jnp.int32, (LONG, PAIR), 1) % HEAD
            at = lax.broadcasted_iota(jnp.int32, (LONG, PAIR), 0)
            segment, valid = segment_limits(i.plan, i.lengths, slab, at)
            s.qfeat[...] = jnp.where(segment == lane, 1.0, 0.0).astype(BF)
            closed = (lane < LONG // SHORT) & ((segment != lane) | jnp.logical_not(valid))
            s.kfeat[...] = jnp.where(closed, MASKED, 0.0).astype(BF)
            copies.wait(*(["left", "right"] if role == 0 else ["left"]))
            hidden = s.h[...]
            copies.wait("wq")
            queries = nn(hidden, s.wq[...]) + i.qb[...].astype(F32)
            s.q[...] = (queries * (FACTOR * LOG2E)).astype(BF)
            store("h")
            store("q")
            copies.wait("wk")
            s.k[...] = nn(hidden, s.wk[...]).astype(BF)
            store("k")
            copies.wait("wv")
            s.v[...] = (nn(hidden, s.wv[...]) + i.vb[...].astype(F32)).astype(BF)
            store("v")
            base = copies.used
            copies.used += PAIRS

            def probs_out(pair):
                two = pl.ds(2 * pair, 2)
                return pltpu.make_async_copy(
                    s.p.at[two], o.p.at[slab, two], copies.sems.at[base + pair]
                )

            def pair_step(pair, carry):
                cols = lane_block(pair, PAIR)
                qp, kp, vp = s.q[:, cols], s.k[:, cols], s.v[:, cols]
                sides = []
                for j in range(2):
                    here = in_half(j)
                    scores = nt(
                        jnp.where(here, qp, s.qfeat[...]), jnp.where(here, kp, s.kfeat[...])
                    )
                    top = jnp.max(scores, axis=1, keepdims=True)
                    raised = jnp.exp2(scores - top).astype(BF)
                    s.p[2 * pair + j] = raised
                    sides.append(nn(raised, jnp.where(here, vp, jnp.ones_like(vp))))
                low = in_half(0)
                rinv = 1.0 / pltpu.roll(jnp.where(low, sides[1], sides[0]), HEAD, 1)
                mix = jnp.where(low, sides[0], sides[1]) * rinv
                s.full[:, cols] = mix
                s.rinv[:, cols] = rinv
                s.att[:, cols] = mix.astype(BF)
                probs_out(pair).start()
                return carry

            lax.fori_loop(0, PAIRS, pair_step, 0, unroll=2)
            for n in ("att", "full", "rinv"):
                store(n)
            copies.wait("wo")
            res = hidden.astype(F32) + (nn(s.att[...], s.wo[...]) + i.ob[...].astype(F32))
            centre = res - row_mean(res)
            rstd1 = lax.rsqrt(row_mean(centre * centre) + EPSILON)
            xhat = centre * rstd1
            normed = xhat * i.g1[...].astype(F32) + i.b1[...].astype(F32)
            s.xh1[...] = xhat.astype(BF)
            s.nl[...] = normed.astype(BF)
            s.normed[...] = normed
            store("xh1")
            store("nl")
            for c in range(chunks):
                cols = lane_block(c, chunk)
                copies.wait(f"up{c}")
                lifted = nn(s.nl[...], s.up[:, cols]) + i.upb[:, cols].astype(F32)
                cdf = 0.5 + 0.5 * lax.erf(lifted * 0.7071067811865476)
                act = (lifted * cdf).astype(BF)
                dens = jnp.exp2(lifted * lifted * (-0.5 * LOG2E)) * 0.3989422804014327
                s.act[:, cols] = act
                s.dg[:, cols] = (cdf + lifted * dens).astype(BF)
                copies.wait(f"down{c}")
                part = nn(act, s.down[cols, :])
                s.acc[...] = part if c == 0 else s.acc[...] + part
                copies.start(f"act{c}", s.act.at[:, cols], o.act.at[slab, :, cols])
                copies.start(f"dg{c}", s.dg.at[:, cols], o.dg.at[slab, :, cols])
            res = s.normed[...] + s.acc[...] + i.downb[...].astype(F32)
            centre = res - row_mean(res)
            rstd2 = lax.rsqrt(row_mean(centre * centre) + EPSILON)
            xhat = centre * rstd2
            s.out[...] = (xhat * i.g2[...].astype(F32) + i.b2[...].astype(F32)).astype(BF)
            copies.start("sent", s.out, o.sent)
            store("out")
            s.xh2[...] = xhat.astype(BF)
            store("xh2")
            side = lax.broadcasted_iota(jnp.int32, (LONG, 128), 1)
            s.st[...] = jnp.where(side < 64, rstd1, rstd2)
            store("st")
            for pair in range(PAIRS):
                probs_out(pair).wait()
            copies.wait_all()

        pl.when(i.section[0] == role)(run)

    made = call(
        "forward_layer", body, dict(section=section, plan=plan, lengths=lengths), vectors, far,
        outs, scratch, 64, 16_000_000_000, kept,
    )
    sent = made.pop("sent")
    return made, sent


def norm_back(grad, xhat, rstd, gain):
    scaled = grad * gain
    return rstd * (scaled - row_mean(scaled) - xhat * row_mean(scaled * xhat))


def backward_slab(
    role, slab, count, phases, scalars, vectors, cots, weights, kept, passed, made, after=(),
    dp_count=0,
):
    do_norm, do_feed, do_attn = (n in phases for n in ("norm", "feed", "attn"))
    wide, deep = kept["h"].shape[2], kept["act"].shape[2]
    rows = (LONG, wide)
    half = wide // 2
    chunk = wide
    chunks = deep // chunk
    stacks, loose = {}, {}
    uses, needs, links = [], [], []
    if do_norm:
        stacks.update(ddown=(rows, BF), vec0=((8, wide), F32))
        uses += ["xh2", "st"]
        if role == 1:
            stacks.update(term=((8, LONG), F32))
            uses += ["out"]
    if do_feed:
        stacks.update(dlift=((LONG, deep), BF), dbranch=(rows, BF), vec1=((8, wide), F32))
        uses += ["dg", "xh1"] + ([] if do_norm else ["st"])
        needs += ["down", "up"]
    if do_attn:
        stacks.update(dqkv=((LONG, 3 * wide), BF), vec2=((8, wide), F32), dh=(rows, BF))
        uses += ["full", "rinv", "q", "k", "v", "p"]
        needs += ["wo", "wq", "wk", "wv"]
        loose.update(sent=(rows, BF))
    if do_norm and not do_feed:
        loose.update(dr2=(rows, F32))
    if do_feed and not do_attn:
        loose.update(dr1=(rows, F32))
    if do_feed and not do_norm:
        links += ["dr2", "ddown"]
    if do_attn and not do_feed:
        links += ["dr1", "dbranch"]
    products, depth = [], 0
    by_parts = dp_count == 16
    if dp_count:
        products += [("act", "ddown")] if do_norm else []
        products += [("nl", "dlift"), ("att", "dbranch")] if do_feed else []
        products += [("h", "dqkv")] if do_attn else []
        depth = kept[products[0][0]].shape[2]
    far = {"r_" + n: kept[n] for n in uses}
    far.update({"w_" + left: kept[left] for left, right in products})
    far.update({n: weights[n] for n in needs})
    far.update({"l_" + n: passed[n] for n in links})
    if do_norm:
        far.update(cots)
    far.update({f"after{n}": array for n, array in enumerate(after)})
    outs = {n: ((count,) + d, k) for n, (d, k) in stacks.items()}
    outs.update(loose)
    scratch = {n: (kept[n].shape[1:], kept[n].dtype) for n in uses}
    scratch.update({n: (weights[n].shape[1:], BF) for n in needs})
    scratch.update(stacks)
    scratch.update(dr2=(rows, F32), dr1=(rows, F32))
    if do_norm:
        scratch.update(cot=(rows, BF))
    if do_feed:
        scratch.update(acc=(rows, F32), ddown=(rows, BF))
    if do_attn:
        scratch.update(datt=(rows, BF), dbranch=(rows, BF))
    if products:
        across = sum(stacks[right][0][1] for left, right in products)
        share = depth // dp_count
        if by_parts:
            scratch.update(grad=((2, dp_count // 2, share, across), BF))
            loose.update(send=((dp_count // 2, share, across), BF))
            loose.update(keep=((dp_count // 2, share, across), BF))
        else:
            scratch.update(grad=((depth, across), BF))
            loose.update(grad=((depth, across), BF))
        outs.update(loose)
        for left, right in products:
            scratch["w_" + left] = ((count * LONG, depth), BF)
            scratch[right] = ((count * LONG, stacks[right][0][1]), BF)

    def body(i, o, s, copies):
        def get(name):
            copies.start("r_" + name, getattr(i, "r_" + name).at[slab], getattr(s, name))

        def get_weight(name):
            copies.start(name, getattr(i, name).at[0], getattr(s, name))

        def put(name):
            copies.start("o" + name, getattr(s, name), getattr(o, name).at[slab])

        def norm_loads():
            if role == 1:
                get("out")
                mine = pl.ds(slab * LONG, LONG)
                copies.start("left", i.other.at[mine], s.cot.at[:, pl.ds(0, half)])
                copies.start("right", i.own.at[mine], s.cot.at[:, pl.ds(half, half)])
            else:
                copies.start("left", i.recv, s.cot)
            get("xh2")
            get("st")

        def feed_loads():
            for c in range(chunks):
                cols = lane_block(c, chunk)
                copies.start(f"down{c}", i.down.at[0, cols, :], s.down.at[cols, :])
                copies.start(f"dg{c}", i.r_dg.at[slab, :, cols], s.dg.at[:, cols])
                copies.start(f"up{c}", i.up.at[0, :, cols], s.up.at[:, cols])
            get("xh1")

        def attn_loads():
            get_weight("wo")
            for n in ("rinv", "full", "v", "k", "q"):
                get(n)
            for pair in range(PAIRS):
                two = pl.ds(2 * pair, 2)
                copies.start(f"p{pair}", i.r_p.at[slab, two], s.p.at[two])
            for n in ("wq", "wk", "wv"):
                get_weight(n)

        def head_phase():
            position = lax.broadcasted_iota(jnp.int32, (LONG, 1), 0)
            valid = segment_limits(i.plan, i.lengths, slab, position)[1]
            valid = jnp.where(valid, 1.0, 0.0)
            cot_row = jnp.broadcast_to(i.weight_cot[slab], (8, LONG))
            cot_column = jnp.transpose(cot_row)[:, :1] * valid
            copies.wait("r_out")
            mixed = s.out[...].astype(F32)
            head = i.head_weight[...].astype(F32)
            pre = jnp.sum(mixed * head, axis=1, keepdims=True) + i.head_bias[0]
            term = jnp.maximum(pre, 0.0) + jnp.log1p(jnp.exp(-jnp.abs(pre)))
            s.term[...] = jnp.transpose(jnp.broadcast_to(term * valid, (LONG, 128)))[:8]
            put("term")
            g_pre = cot_column / (1.0 + jnp.exp(-pre))
            s.vec0[3:4, :] = column_sum(g_pre * mixed)
            s.vec0[4:5, :] = jnp.broadcast_to(column_sum(g_pre), (1, wide))
            copies.wait("left", "right")
            return s.cot[...].astype(F32) + g_pre * head

        def norm_phase():
            if role == 1:
                grad = head_phase()
            else:
                copies.wait("left")
                grad = s.cot[...].astype(F32)
            copies.wait("r_xh2", "r_st")
            xhat = s.xh2[...].astype(F32)
            s.vec0[0:1, :] = column_sum(grad * xhat)
            s.vec0[1:2, :] = column_sum(grad)
            dr2 = norm_back(grad, xhat, s.st[:, 64:65], i.g2[...].astype(F32))
            s.dr2[...] = dr2
            s.ddown[...] = dr2.astype(BF)
            put("ddown")
            s.vec0[2:3, :] = column_sum(s.ddown[...])
            put("vec0")

        def feed_phase():
            for c in range(chunks):
                cols = lane_block(c, chunk)
                copies.wait(f"down{c}", f"dg{c}")
                dact = nt(s.ddown[...], s.down[cols, :])
                dlift = (dact * s.dg[:, cols].astype(F32)).astype(BF)
                s.dlift[:, cols] = dlift
                s.vec1[3 + c : 4 + c, :] = column_sum(dlift)
                copies.wait(f"up{c}")
                part = nt(dlift, s.up[:, cols])
                s.acc[...] = part if c == 0 else s.acc[...] + part
                copies.start(f"dlift{c}", s.dlift.at[:, cols], o.dlift.at[slab, :, cols])
            copies.wait("r_xh1")
            dnormed = s.dr2[...] + s.acc[...]
            xhat = s.xh1[...].astype(F32)
            s.vec1[0:1, :] = column_sum(dnormed * xhat)
            s.vec1[1:2, :] = column_sum(dnormed)
            dr1 = norm_back(dnormed, xhat, s.st[:, 0:1], i.g1[...].astype(F32))
            s.dr1[...] = dr1
            s.dbranch[...] = dr1.astype(BF)
            put("dbranch")
            s.vec1[2:3, :] = column_sum(s.dbranch[...])
            put("vec1")

        def attn_phase():
            copies.wait("wo")
            s.datt[...] = nt(s.dbranch[...], s.wo[...]).astype(BF)
            copies.wait("r_rinv", "r_full", "r_v", "r_k", "r_q")
            waits = [copies.named.pop(f"p{pair}") for pair in range(PAIRS)]
            for pair in range(PAIRS):
                waits[pair].wait()

            def pair_step(pair, carry):
                cols = lane_block(pair, PAIR)
                qp, kp, vp = s.q[:, cols], s.k[:, cols], s.v[:, cols]
                scaled = (s.datt[:, cols].astype(F32) * s.rinv[:, cols]).astype(BF)
                joint = scaled.astype(F32) * s.full[:, cols]
                parts = []
                for j in range(2):
                    here = in_half(j)
                    own = jnp.where(here, scaled, jnp.zeros_like(scaled))
                    delta = jnp.sum(jnp.where(here, joint, 0.0), axis=1, keepdims=True)
                    raised = s.p[2 * pair + j]
                    dscores = (raised.astype(F32) * (nt(own, vp) - delta)).astype(BF)
                    parts.append((nn(dscores, kp), tn(dscores, qp), tn(raised, scaled)))
                low = in_half(0)
                dq, dk, dv = (jnp.where(low, a, b) for a, b in zip(*parts))
                s.dqkv[:, cols] = (dq.astype(BF).astype(F32) * FACTOR).astype(BF)
                s.dqkv[:, lane_block(pair + PAIRS, PAIR)] = (dk * LN2).astype(BF)
                s.dqkv[:, lane_block(pair + 2 * PAIRS, PAIR)] = dv.astype(BF)
                return carry

            lax.fori_loop(0, PAIRS, pair_step, 0, unroll=2)
            put("dqkv")
            total = s.dr1[...]
            for n, name in enumerate(("wq", "wk", "wv")):
                copies.wait(name)
                total = total + nt(s.dqkv[:, lane_block(n, wide)], getattr(s, name)[...])
            s.dh[...] = total.astype(BF)
            copies.start("sent", s.dh, o.sent)
            put("dh")
            s.vec2[0:1, :] = column_sum(s.dqkv[:, lane_block(0, wide)])
            s.vec2[1:2, :] = column_sum(s.dqkv[:, lane_block(2, wide)])
            put("vec2")

        def product_loads():
            for left, right in products:
                wide_left, wide_right = getattr(s, "w_" + left), getattr(s, right)
                setattr(s, "all_" + right, wide_right)
                setattr(s, right, wide_right.at[pl.ds(slab * LONG, LONG)])
                for t in range(count):
                    at = pl.ds(t * LONG, LONG)
                    copies.start(f"w{left}{t}", getattr(i, "w_" + left).at[t], wide_left.at[at])
                    if t != slab:
                        copies.start(
                            f"w{right}{t}", getattr(o, right).at[t], wide_right.at[at]
                        )
            return [copies.named.pop(f"w{left}{t}") for left, _ in products for t in range(count)] + [
                copies.named.pop(f"w{right}{t}")
                for _, right in products
                for t in range(count)
                if t != slab
            ]

        def product_phase(waits):
            made_here = [
                copies.make("m" + right, getattr(o, right).at[slab], getattr(s, right))
                for _, right in products
            ]
            for _, right in products:
                copies.named.pop("m" + right)

            def fetch():
                for copy in made_here:
                    copy.start()
                for copy in made_here:
                    copy.wait()

            pl.when(i.section[0] != role)(fetch)
            for copy in waits:
                copy.wait()
            step, base = wide, 0
            for left, right in products:
                whole_left, whole_right = getattr(s, "w_" + left), getattr(s, "all_" + right)
                width = whole_right.shape[1]
                for m in range(0, depth, step):
                    for n in range(0, width, step):
                        part = tn(
                            whole_left[:, m : m + step], whole_right[:, n : n + step]
                        ).astype(BF)
                        cols = pl.ds(base + n, step)
                        if not by_parts:
                            s.grad[m : m + step, cols] = part
                            continue
                        for j in range(m // share, (m + step) // share):
                            other_core = jnp.where(i.core[0] == j % 2, 0, 1)
                            at = j * share - m
                            s.grad[other_core, j // 2, :, cols] = part[at : at + share]
                    if not by_parts:
                        continue
                if by_parts:
                    cols = pl.ds(base, width)
                    copies.start("keep" + left, s.grad.at[0, :, :, cols], o.keep.at[:, :, cols])
                    copies.start("send" + left, s.grad.at[1, :, :, cols], o.send.at[:, :, cols])
                base += width
            if not by_parts:
                copies.start("grad", s.grad, o.grad)
            copies.wait_all()

        def run():
            if do_norm:
                norm_loads()
            if do_feed and not do_norm:
                get("st")
            for n in links:
                far_ref = getattr(i, "l_" + n)
                copies.start(
                    "l_" + n, far_ref if n in ("dr1", "dr2") else far_ref.at[slab], getattr(s, n)
                )
            if do_feed:
                feed_loads()
            elif do_attn:
                attn_loads()
            if do_norm:
                norm_phase()
            if do_feed and do_attn:
                attn_loads()
            copies.wait(*["l_" + n for n in links])
            if do_feed:
                if not do_norm:
                    copies.wait("r_st")
                feed_phase()
            if do_attn:
                attn_phase()
            for n in loose:
                if n in ("dr1", "dr2"):
                    copies.start("o" + n, getattr(s, n), getattr(o, n))
            copies.wait_all()

        waits = product_loads() if products else []
        pl.when(i.section[0] == role)(run)
        if products:
            product_phase(waits)

    local = {}
    if do_norm:
        names = ("head_weight", "weight_cot", "g2") if role == 1 else ("g2",)
        local.update({n: vectors[n] for n in names})
    if do_feed:
        local.update(g1=vectors["g1"])
    result = call(
        "backward_" + "_".join(phases), body, scalars, local, far, outs, scratch, 88,
        6_000_000_000 * len(phases), {n: made[n] for n in stacks} if made else None,
    )
    return dict(made or {}, **{n: result[n] for n in stacks}), {n: result[n] for n in loose}


def pick(array_in, index, axis):
    return lax.dynamic_index_in_dim(array_in, index, axis, keepdims=False)


def cut(array_in, start, size):
    return lax.dynamic_slice_in_dim(array_in, start, size, 0)


def added(*pieces):
    total = pieces[0].astype(F32)
    for piece in pieces[1:]:
        total = total + piece.astype(F32)
    return total


def routed(block, pairs):
    return lax.ppermute(block, "dp", pairs)


def swap_bit(block, bit):
    return routed(block, [(i, i ^ bit) for i in range(lax.axis_size("dp"))])


def behind(array_in, *others):
    return lax.optimization_barrier((array_in,) + others)[0]


def join(mine, got, start, cost):
    def kernel(start_ref, mine_ref, got_ref, sum_ref, send_ref):
        for j in range(4):
            sum_ref[j] = added(mine_ref[j], got_ref[j]).astype(BF)
        for j in range(3):
            send_ref[j] = sum_ref[start_ref[0] + j]

    local = pl.BlockSpec(memory_space=pltpu.VMEM)
    return pl.pallas_call(
        kernel,
        out_shape=[
            jax.ShapeDtypeStruct(mine.shape, BF),
            jax.ShapeDtypeStruct((3,) + mine.shape[1:], BF),
        ],
        in_specs=[pl.BlockSpec(memory_space=pltpu.SMEM), local, local],
        out_specs=[local, local],
        compiler_params=pltpu.CompilerParams(vmem_limit_bytes=32 << 20),
        cost_estimate=pl.CostEstimate(flops=cost, bytes_accessed=8_000_000, transcendentals=0),
        name="join_quarters",
    )(start, mine, got)


class ShardSum:
    def __init__(self, made):
        self.by_parts = "send" in made
        if not self.by_parts:
            self.grad = made["grad"]
            self.mark = (self.grad,)
            return
        me = lax.axis_index("dp")
        self.side, self.place = (me // 2) % 2, me // 4
        self.lower = self.place <= 1
        in_lines = lambda array: array.reshape((4, 2) + array.shape[1:])
        self.mine, self.got = in_lines(made["keep"]), swap_bit(in_lines(made["send"]), 1)
        self.mark = (made["send"],)

    def step(self, run, *before):
        if self.by_parts:
            if before:
                self.got = behind(self.got, *before)
            self.mark = (run(),)
        return self

    def to_line(self, *before):
        def run():
            mine, got, side = self.mine, self.got, self.side
            send = added(pick(mine, 1 - side, 1), pick(got, 1 - side, 1)).astype(BF)
            self.keep = added(pick(mine, side, 1), pick(got, side, 1)).astype(BF)
            self.got = swap_bit(send, 2)
            return send

        return self.step(run, *before)

    def inwards(self, *before, cost=1_000_000_000):
        def run():
            start = jnp.where(self.place == 0, 1, 0).astype(jnp.int32)[None]
            self.blocks, send = join(self.keep, self.got, start, cost)
            row = range(4)
            self.got = routed(send, [(j, j + 4) for j in row] + [(j + 12, j + 8) for j in row])
            return send

        return self.step(run, *before)

    def across(self, *before):
        def run():
            lower, row = self.lower, range(4)
            self.ends = self.got
            send = added(
                cut(self.blocks, jnp.where(lower, 2, 0), 2),
                cut(self.ends, jnp.where(lower, 1, 0), 2),
            ).astype(BF)
            self.got = routed(send, [(j + 4, j + 8) for j in row] + [(j + 8, j + 4) for j in row])
            return send

        return self.step(run, *before)

    def outwards(self, *before):
        def run():
            lower, row = self.lower, range(4)
            self.middle = self.got
            send = added(
                pick(self.blocks, jnp.where(lower, 0, 3), 0),
                pick(self.middle, jnp.where(lower, 0, 1), 0),
            ).astype(BF)
            self.got = routed(send, [(j + 4, j) for j in row] + [(j + 8, j + 12) for j in row])
            return send

        return self.step(run, *before)

    def last(self, *before):
        if not self.by_parts:
            return lax.psum_scatter(
                self.grad.astype(F32), "dp", scatter_dimension=0, tiled=True
            )
        got = behind(self.got, *before) if before else self.got
        total = added(
            pick(self.blocks, self.place, 0),
            pick(self.ends, jnp.where(self.lower, 0, 2), 0),
            pick(self.middle, jnp.where(self.lower, 1, 0), 0),
            got,
        )
        self.mark = (total,)
        return total


def body(
    tokens,
    out_cot,
    weight_cot,
    plan,
    lengths,
    q_weight,
    k_weight,
    v_weight,
    o_weight,
    q_bias,
    v_bias,
    o_bias,
    norm1_gain,
    norm1_bias,
    up_weight,
    up_bias,
    down_weight,
    down_bias,
    norm2_gain,
    norm2_bias,
    head_weight,
    head_bias,
):
    my_section = lax.axis_index("pipe")
    is_first = my_section == 0
    section = my_section.astype(jnp.int32)[None]
    row_count, half = tokens.shape
    wide, deep = up_weight.shape[1:]
    count = row_count // LONG
    dp_count = lax.axis_size("dp")
    share = wide // dp_count
    to_next, to_back = [(0, 1)], [(1, 0)]
    slab_of = lambda array, j: array[j * LONG : (j + 1) * LONG]
    over = lambda array, way: lax.ppermute(array, "pipe", way)
    token_other = [over(slab_of(tokens, j), to_back) for j in range(count)]
    cot_other = over(out_cot, to_next)
    weights = dict(
        wq=q_weight, wk=k_weight, wv=v_weight, wo=o_weight, up=up_weight, down=down_weight
    )
    vectors = dict(
        qb=q_bias, vb=v_bias, ob=o_bias, g1=norm1_gain, b1=norm1_bias, upb=up_bias,
        downb=down_bias, g2=norm2_gain, b2=norm2_bias,
    )
    kept, recv = None, []
    for j in range(count):
        kept, sent = forward_slab(
            0, j, count, section, plan, lengths, tokens, token_other[j], None, weights, vectors,
            kept, [cot_other] if j else [],
        )
        recv.append(over(sent, to_next))
    mixed_got = []
    for j in range(count):
        kept, sent = forward_slab(
            1, j, count, section, plan, lengths, None, None, recv[j], weights, vectors, kept, []
        )
        mixed_got.append(over(sent[:, :half], to_back))
    scalars = dict(section=section, plan=plan, lengths=lengths, head_bias=head_bias)
    vectors = dict(
        g1=norm1_gain, g2=norm2_gain, head_weight=head_weight[None],
        weight_cot=weight_cot.reshape(count, 1, LONG),
    )
    full = ("norm", "feed", "attn")
    made, recv = None, [None] * count
    for j in reversed(range(count)):
        made, loose = backward_slab(
            1, j, count, full, scalars, vectors, dict(own=out_cot, other=cot_other), weights, kept,
            {}, made, [mixed_got[count - 1 - j]],
        )
        recv[j] = over(loose["sent"], to_back)
    token_got = [None] * count
    for j in reversed(range(1, count)):
        made, loose = backward_slab(
            0, j, count, full, scalars, vectors, dict(recv=recv[j]), weights, kept, {}, made
        )
        token_got[j] = over(loose["sent"][:, half:], to_next)
    head_sums = jnp.sum(made["vec0"][:, 3:5], axis=0)
    term = made["term"][:, 0].reshape(row_count)
    early = jnp.concatenate([term, head_sums[0], head_sums[1, :1]])
    early_got = over(early, to_back)
    early = jnp.where(is_first, early_got, early)
    scalars["core"] = (lax.axis_index("dp") % 2).astype(jnp.int32)[None]
    last = functools.partial(backward_slab, 0, 0, count)
    made, loose = last(
        ("norm",), scalars, vectors, dict(recv=recv[0]), weights, kept, {}, made, [early_got],
        dp_count,
    )
    down_sum = ShardSum(loose).to_line()
    made, loose = last(
        ("feed",), scalars, vectors, {}, weights, kept, dict(loose, ddown=made["ddown"]), made,
        down_sum.mark, dp_count,
    )
    feed_sum = ShardSum(loose)
    down_sum.inwards(*feed_sum.mark, cost=60_000_000_000)
    feed_sum.to_line(*down_sum.mark)
    made, loose = last(
        ("attn",), scalars, vectors, {}, weights, kept, dict(loose, dbranch=made["dbranch"]), made,
        feed_sum.mark + down_sum.mark, dp_count,
    )
    qkv_sum = ShardSum(loose)
    token_got[0] = over(loose["sent"][:, half:], to_next)
    down_sum.across(*qkv_sum.mark)
    sums0, sums1, sums2 = (
        jnp.sum(behind(made[n], *down_sum.mark), axis=0) for n in ("vec0", "vec1", "vec2")
    )
    lines = jnp.concatenate(
        [sums2[:2], sums1[2:3], sums1[:2], sums0[2:3], sums0[:2], early[None, row_count:-1]]
    )
    flat = jnp.concatenate(
        [
            lines.reshape(9, dp_count, share).transpose(1, 0, 2).reshape(dp_count, -1),
            sums1[3 : 3 + deep // wide].reshape(dp_count, -1),
            jnp.broadcast_to(early[None, -1:], (dp_count, 1)),
        ],
        axis=1,
    )
    if qkv_sum.by_parts:
        flat = flat + swap_bit(flat, 1)
    feed_sum.inwards(*down_sum.mark)
    qkv_sum.to_line(*feed_sum.mark)
    if qkv_sum.by_parts:
        flat = behind(flat, *qkv_sum.mark)
        flat = flat + swap_bit(flat, 2)
    down_sum.outwards(*qkv_sum.mark)
    feed_sum.across(*down_sum.mark)
    if qkv_sum.by_parts:
        flat = behind(flat, *feed_sum.mark)
        flat = flat + swap_bit(flat, 4)
    qkv_sum.inwards(*feed_sum.mark)
    down_grad = down_sum.last(*qkv_sum.mark)
    feed_sum.outwards(*down_sum.mark)
    if qkv_sum.by_parts:
        flat = behind(flat, *feed_sum.mark)
        flat = flat + swap_bit(flat, 8)
        flat = pick(flat, lax.axis_index("dp"), 0)
    else:
        flat = lax.psum_scatter(flat, "dp", scatter_dimension=0, tiled=True)[0]
    qkv_sum.across(*feed_sum.mark)
    feed_grad = feed_sum.last(*qkv_sum.mark)
    qkv_sum.outwards(*feed_sum.mark)
    qkv_grad = qkv_sum.last()
    up_grad, o_grad = feed_grad[:, :deep], feed_grad[:, deep:]
    at = lambda j: flat[j * share : (j + 1) * share]
    out_rows = kept["out"].reshape(row_count, wide)
    grad_rows = made["dh"].reshape(row_count, wide)
    mixed_out = jnp.where(is_first, jnp.concatenate(mixed_got), out_rows[:, half:])
    tokens_grad = jnp.where(is_first, grad_rows[:, :half], jnp.concatenate(token_got))
    return (
        mixed_out,
        early[:row_count],
        tokens_grad,
        qkv_grad[None, :, :wide],
        qkv_grad[None, :, wide : 2 * wide],
        qkv_grad[None, :, 2 * wide :],
        o_grad[None],
        at(0)[None],
        at(1)[None],
        at(2)[None],
        at(3)[None],
        at(4)[None],
        up_grad[None],
        flat[None, 9 * share : 9 * share + deep // dp_count],
        down_grad[None],
        at(5)[None],
        at(6)[None],
        at(7)[None],
        at(8),
        flat[-1:],
    )


def solution(mesh):
    rows, stack, flat = P("dp", "pipe"), P("pipe", None, None), P("pipe", None)
    in_specs = (
        (rows, rows, P("dp"), P("dp"), P("dp", None))
        + (stack,) * 4
        + (flat,) * 5
        + (stack, flat, stack, flat, flat, flat, P(), P())
    )
    shard, line = P("pipe", "dp", None), P("pipe", "dp")
    out_specs = (
        (rows, P("dp"), rows)
        + (shard,) * 4
        + (line,) * 5
        + (shard, line, shard, line, line, line, P("dp"), P())
    )
    return jax.shard_map(body, mesh=mesh, in_specs=in_specs, out_specs=out_specs, check_vma=False)
```

```python
import functools
from types import SimpleNamespace

import jax
import jax.numpy as jnp
from jax import lax
from jax.experimental import pallas as pl
from jax.experimental.pallas import tpu as pltpu
from jax.sharding import PartitionSpec as P

HEADS = 12
HEAD = 64
PAIR = 2 * HEAD
PAIRS = HEADS // 2
SHORT = 128
LONG = 512
EPSILON = 1e-06
MASKED = -1e30
FACTOR = HEAD**-0.5
LOG2E = 1.4426950408889634
LN2 = 0.6931471805599453
BF = jnp.bfloat16
F32 = jnp.float32
VMEM_BYTES = 58 << 20


def product(dims, left_side, right_side):
    return lax.dot_general(left_side, right_side, (dims, ((), ())), preferred_element_type=F32)


nn = functools.partial(product, ((1,), (0,)))
nt = functools.partial(product, ((1,), (1,)))
tn = functools.partial(product, ((0,), (0,)))


def segment_limits(plan, lengths, slab, position):
    is_long = plan[slab] == 1
    parts = [lengths[slab, j] for j in range(LONG // SHORT)]
    slot = position // SHORT
    own = jnp.full(position.shape, parts[-1], jnp.int32)
    for j in range(len(parts) - 1):
        own = jnp.where(slot == j, parts[j], own)
    limit = jnp.where(is_long, sum(parts), own + slot * SHORT)
    return jnp.where(is_long, 0, slot), position < limit


def row_mean(rows_in):
    return jnp.mean(rows_in, axis=1, keepdims=True)


def column_sum(rows_in):
    return jnp.sum(rows_in.astype(F32), axis=0, keepdims=True)


def in_half(j):
    lane = lax.broadcasted_iota(jnp.int32, (LONG, PAIR), 1)
    return (lane < HEAD) if j == 0 else (lane >= HEAD)


def lane_block(index, width):
    start = index * width
    return pl.ds(start if isinstance(index, int) else pl.multiple_of(start, width), width)


class Copies:
    def __init__(self, sems):
        self.sems, self.used, self.named = sems, 0, {}

    def make(self, name, src, dst):
        copy = pltpu.make_async_copy(src, dst, self.sems.at[self.used])
        self.used += 1
        self.named[name] = copy
        return copy

    def start(self, name, src, dst):
        self.make(name, src, dst).start()

    def wait(self, *names):
        for name in names:
            self.named.pop(name).wait()

    def wait_all(self):
        self.wait(*list(self.named))


def call(name, body, scalars, local, far, outs, scratch, sems, cost, kept=None):
    kept = kept or {}
    names = list(scalars) + list(local) + list(far)
    arrays = list(scalars.values()) + list(local.values()) + list(far.values())
    specs = [pl.BlockSpec(memory_space=pltpu.SMEM)] * len(scalars)
    specs += [pl.BlockSpec(memory_space=pltpu.VMEM)] * len(local)
    specs += [pl.BlockSpec(memory_space=pl.ANY)] * (len(far) + len(kept))
    aliases = {}
    for key, array in kept.items():
        aliases[len(arrays)] = list(outs).index(key)
        arrays.append(array)
    skip = len(kept)

    def kernel(*refs):
        refs = list(refs)
        given, rest = refs[: len(names)], refs[len(names) + skip :]
        n = len(outs)
        body(
            SimpleNamespace(**dict(zip(names, given))),
            SimpleNamespace(**dict(zip(outs, rest[:n]))),
            SimpleNamespace(**dict(zip(scratch, rest[n : n + len(scratch)]))),
            Copies(rest[-1]),
        )

    made = pl.pallas_call(
        kernel,
        out_shape=[jax.ShapeDtypeStruct(d, k) for d, k in outs.values()],
        in_specs=specs,
        out_specs=[pl.BlockSpec(memory_space=pl.ANY)] * len(outs),
        scratch_shapes=[pltpu.VMEM(d, k) for d, k in scratch.values()]
        + [pltpu.SemaphoreType.DMA((sems,))],
        input_output_aliases=aliases,
        compiler_params=pltpu.CompilerParams(vmem_limit_bytes=VMEM_BYTES),
        cost_estimate=pl.CostEstimate(flops=cost, bytes_accessed=30_000_000, transcendentals=0),
        name=name,
    )(*arrays)
    return dict(zip(outs, made))


def forward_slab(
    role, slab, count, section, plan, lengths, own, other, recv, weights, vectors, kept, after
):
    wide, deep = weights["wq"].shape[1], weights["up"].shape[2]
    half = wide // 2
    rows = (LONG, wide)
    stack = {
        "h": (rows, BF), "q": (rows, BF), "k": (rows, BF), "v": (rows, BF),
        "p": ((HEADS, LONG, LONG), BF), "att": (rows, BF), "full": (rows, F32),
        "rinv": (rows, F32), "xh1": (rows, BF), "nl": (rows, BF), "act": ((LONG, deep), BF),
        "dg": ((LONG, deep), BF), "xh2": (rows, BF), "st": ((LONG, 128), F32), "out": (rows, BF),
    }
    outs = {n: ((count,) + d, k) for n, (d, k) in stack.items()}
    outs["sent"] = (rows if role == 0 else (LONG, half), BF)
    scratch = dict(stack)
    scratch.update({n: (w.shape[1:], BF) for n, w in weights.items()})
    scratch.update({
        "normed": (rows, F32), "acc": (rows, F32), "qfeat": ((LONG, PAIR), BF),
        "kfeat": ((LONG, PAIR), BF),
    })
    far = dict(weights)
    far.update(dict(own=own, other=other) if role == 0 else dict(recv=recv))
    far.update({f"after{n}": array for n, array in enumerate(after)})
    chunk = wide
    chunks = deep // chunk

    def body(i, o, s, copies):
        def run():
            if role == 0:
                mine = pl.ds(slab * LONG, LONG)
                copies.start("left", i.own.at[mine], s.h.at[:, pl.ds(0, half)])
                copies.start("right", i.other, s.h.at[:, pl.ds(half, half)])
            else:
                copies.start("left", i.recv, s.h)
            for n in ("wq", "wk", "wv"):
                copies.start(n, getattr(i, n).at[0], getattr(s, n))

            def rest_loads():
                copies.start("wo", i.wo.at[0], s.wo)
                for c in range(chunks):
                    cols = lane_block(c, chunk)
                    copies.start(f"up{c}", i.up.at[0, :, cols], s.up.at[:, cols])
                    copies.start(f"down{c}", i.down.at[0, cols, :], s.down.at[cols, :])

            def store(name):
                copies.start("o" + name, getattr(s, name), getattr(o, name).at[slab])

            lane = lax.broadcasted_iota(jnp.int32, (LONG, PAIR), 1) % HEAD
            at = lax.broadcasted_iota(jnp.int32, (LONG, PAIR), 0)
            segment, valid = segment_limits(i.plan, i.lengths, slab, at)
            s.qfeat[...] = jnp.where(segment == lane, 1.0, 0.0).astype(BF)
            closed = (lane < LONG // SHORT) & ((segment != lane) | jnp.logical_not(valid))
            s.kfeat[...] = jnp.where(closed, MASKED, 0.0).astype(BF)
            copies.wait(*(["left", "right"] if role == 0 else ["left"]))
            hidden = s.h[...]
            copies.wait("wq", "wk", "wv")
            rest_loads()
            queries = nn(hidden, s.wq[...]) + i.qb[...].astype(F32)
            s.q[...] = (queries * (FACTOR * LOG2E)).astype(BF)
            s.k[...] = nn(hidden, s.wk[...]).astype(BF)
            store("h")
            store("q")
            store("k")
            s.v[...] = (nn(hidden, s.wv[...]) + i.vb[...].astype(F32)).astype(BF)
            store("v")
            base = copies.used
            copies.used += PAIRS

            def probs_out(pair):
                two = pl.ds(2 * pair, 2)
                return pltpu.make_async_copy(
                    s.p.at[two], o.p.at[slab, two], copies.sems.at[base + pair]
                )

            def pair_step(pair, carry):
                cols = lane_block(pair, PAIR)
                qp, kp, vp = s.q[:, cols], s.k[:, cols], s.v[:, cols]
                sides = []
                for j in range(2):
                    here = in_half(j)
                    scores = nt(
                        jnp.where(here, qp, s.qfeat[...]), jnp.where(here, kp, s.kfeat[...])
                    )
                    top = jnp.max(scores, axis=1, keepdims=True)
                    raised = jnp.exp2(scores - top).astype(BF)
                    s.p[2 * pair + j] = raised
                    sides.append(nn(raised, jnp.where(here, vp, jnp.ones_like(vp))))
                low = in_half(0)
                rinv = 1.0 / pltpu.roll(jnp.where(low, sides[1], sides[0]), HEAD, 1)
                mix = jnp.where(low, sides[0], sides[1]) * rinv
                s.full[:, cols] = mix
                s.rinv[:, cols] = rinv
                s.att[:, cols] = mix.astype(BF)
                probs_out(pair).start()
                return carry

            lax.fori_loop(0, PAIRS, pair_step, 0, unroll=3)
            for n in ("att", "full", "rinv"):
                store(n)
            copies.wait("wo")
            res = hidden.astype(F32) + (nn(s.att[...], s.wo[...]) + i.ob[...].astype(F32))
            centre = res - row_mean(res)
            rstd1 = lax.rsqrt(row_mean(centre * centre) + EPSILON)
            xhat = centre * rstd1
            normed = xhat * i.g1[...].astype(F32) + i.b1[...].astype(F32)
            s.xh1[...] = xhat.astype(BF)
            s.nl[...] = normed.astype(BF)
            s.normed[...] = normed
            store("xh1")
            store("nl")
            copies.wait(*[f"{n}{c}" for n in ("up", "down") for c in range(chunks)])
            for c in range(chunks):
                cols = lane_block(c, chunk)
                lifted = nn(s.nl[...], s.up[:, cols]) + i.upb[:, cols].astype(F32)
                cdf = 0.5 + 0.5 * lax.erf(lifted * 0.7071067811865476)
                act = (lifted * cdf).astype(BF)
                dens = jnp.exp2(lifted * lifted * (-0.5 * LOG2E)) * 0.3989422804014327
                s.act[:, cols] = act
                s.dg[:, cols] = (cdf + lifted * dens).astype(BF)
                part = nn(act, s.down[cols, :])
                s.acc[...] = part if c == 0 else s.acc[...] + part
                copies.start(f"act{c}", s.act.at[:, cols], o.act.at[slab, :, cols])
                copies.start(f"dg{c}", s.dg.at[:, cols], o.dg.at[slab, :, cols])
            res = s.normed[...] + s.acc[...] + i.downb[...].astype(F32)
            centre = res - row_mean(res)
            rstd2 = lax.rsqrt(row_mean(centre * centre) + EPSILON)
            xhat = centre * rstd2
            s.out[...] = (xhat * i.g2[...].astype(F32) + i.b2[...].astype(F32)).astype(BF)
            copies.start("sent", s.out if role == 0 else s.out.at[:, pl.ds(0, half)], o.sent)
            store("out")
            s.xh2[...] = xhat.astype(BF)
            store("xh2")
            side = lax.broadcasted_iota(jnp.int32, (LONG, 128), 1)
            s.st[...] = jnp.where(side < 64, rstd1, rstd2)
            store("st")
            for pair in range(PAIRS):
                probs_out(pair).wait()
            copies.wait_all()

        pl.when(i.section[0] == role)(run)

    made = call(
        "forward_layer", body, dict(section=section, plan=plan, lengths=lengths), vectors, far,
        outs, scratch, 64, 16_000_000_000, kept,
    )
    sent = made.pop("sent")
    return made, sent


def norm_back(grad, xhat, rstd, gain):
    scaled = grad * gain
    return rstd * (scaled - row_mean(scaled) - xhat * row_mean(scaled * xhat))


def backward_slab(
    role, slab, count, phases, scalars, vectors, cots, weights, kept, passed, made, after=(),
    dp_count=0,
):
    do_norm, do_feed, do_attn = (n in phases for n in ("norm", "feed", "attn"))
    wide, deep = kept["h"].shape[2], kept["act"].shape[2]
    rows = (LONG, wide)
    half = wide // 2
    chunk = wide
    chunks = deep // chunk
    stacks, loose = {}, {}
    uses, needs, links = [], [], []
    if do_norm:
        stacks.update(ddown=(rows, BF), vec0=((8, wide), F32))
        uses += ["xh2", "st"]
        if role == 1:
            stacks.update(term=((8, LONG), F32))
            uses += ["out"]
    if do_feed:
        stacks.update(dlift=((LONG, deep), BF), dbranch=(rows, BF), vec1=((8, wide), F32))
        uses += ["dg", "xh1"] + ([] if do_norm else ["st"])
        needs += ["down", "up"]
    if do_attn:
        stacks.update(dqkv=((LONG, 3 * wide), BF), vec2=((8, wide), F32), dh=(rows, BF))
        uses += ["full", "rinv", "q", "k", "v", "p"]
        needs += ["wo", "wq", "wk", "wv"]
        loose.update(sent=(rows if role == 1 else (LONG, half), BF))
    if do_norm and not do_feed:
        loose.update(dr2=(rows, F32))
    if do_feed and not do_attn:
        loose.update(dr1=(rows, F32))
    if do_feed and not do_norm:
        links += ["dr2", "ddown"]
    if do_attn and not do_feed:
        links += ["dr1", "dbranch"]
    products, depth = [], 0
    by_parts = dp_count == 16
    if dp_count:
        products += [("act", "ddown")] if do_norm else []
        products += [("nl", "dlift"), ("att", "dbranch")] if do_feed else []
        products += [("h", "dqkv")] if do_attn else []
        depth = kept[products[0][0]].shape[2]
    far = {"r_" + n: kept[n] for n in uses}
    far.update({"w_" + left: kept[left] for left, right in products})
    far.update({n: weights[n] for n in needs})
    far.update({"l_" + n: passed[n] for n in links})
    if do_norm:
        far.update(cots)
    far.update({f"after{n}": array for n, array in enumerate(after)})
    outs = {n: ((count,) + d, k) for n, (d, k) in stacks.items()}
    outs.update(loose)
    scratch = {n: (kept[n].shape[1:], kept[n].dtype) for n in uses}
    scratch.update({n: (weights[n].shape[1:], BF) for n in needs})
    scratch.update(stacks)
    scratch.update(dr2=(rows, F32), dr1=(rows, F32))
    if do_norm:
        scratch.update(cot=(rows, BF))
    if do_feed:
        scratch.update(acc=(rows, F32), ddown=(rows, BF))
    if do_attn:
        scratch.update(datt=(rows, BF), dbranch=(rows, BF))
    if products:
        across = sum(stacks[right][0][1] for left, right in products)
        share = depth // dp_count
        if by_parts:
            scratch.update(grad=((2, dp_count // 2, share, across), BF))
            loose.update(send=((dp_count // 2, share, across), BF))
            loose.update(keep=((dp_count // 2, share, across), BF))
        else:
            scratch.update(grad=((depth, across), BF))
            loose.update(grad=((depth, across), BF))
        outs.update(loose)
        for left, right in products:
            scratch["w_" + left] = ((count * LONG, depth), BF)
            scratch[right] = ((count * LONG, stacks[right][0][1]), BF)

    def body(i, o, s, copies):
        probs_sems = copies.sems.at[pl.ds(0, PAIRS)]
        copies.used = PAIRS

        def get(name):
            copies.start("r_" + name, getattr(i, "r_" + name).at[slab], getattr(s, name))

        def get_weight(name):
            copies.start(name, getattr(i, name).at[0], getattr(s, name))

        def put(name):
            copies.start("o" + name, getattr(s, name), getattr(o, name).at[slab])

        def norm_loads():
            if role == 1:
                get("out")
                mine = pl.ds(slab * LONG, LONG)
                copies.start("left", i.other.at[mine], s.cot.at[:, pl.ds(0, half)])
                copies.start("right", i.own.at[mine], s.cot.at[:, pl.ds(half, half)])
            else:
                copies.start("left", i.recv, s.cot)
            get("xh2")
            get("st")

        def feed_loads(c):
            cols = lane_block(c, chunk)
            copies.start(f"down{c}", i.down.at[0, cols, :], s.down.at[cols, :])
            copies.start(f"dg{c}", i.r_dg.at[slab, :, cols], s.dg.at[:, cols])
            copies.start(f"up{c}", i.up.at[0, :, cols], s.up.at[:, cols])
            if c == chunks - 1:
                get("xh1")

        def attn_loads():
            get_weight("wo")
            for n in ("rinv", "full", "v", "k", "q"):
                get(n)

        def probs_in(pair):
            two = pl.ds(2 * pair, 2)
            return pltpu.make_async_copy(i.r_p.at[slab, two], s.p.at[two], probs_sems.at[pair])

        def late_loads():
            for pair in range(PAIRS):
                probs_in(pair).start()
            for n in ("wq", "wk", "wv"):
                get_weight(n)

        def head_phase():
            position = lax.broadcasted_iota(jnp.int32, (LONG, 1), 0)
            valid = segment_limits(i.plan, i.lengths, slab, position)[1]
            valid = jnp.where(valid, 1.0, 0.0)
            cot_row = jnp.broadcast_to(i.weight_cot[slab], (8, LONG))
            cot_column = jnp.transpose(cot_row)[:, :1] * valid
            copies.wait("r_out")
            mixed = s.out[...].astype(F32)
            head = i.head_weight[...].astype(F32)
            pre = jnp.sum(mixed * head, axis=1, keepdims=True) + i.head_bias[0]
            term = jnp.maximum(pre, 0.0) + jnp.log1p(jnp.exp(-jnp.abs(pre)))
            s.term[...] = jnp.transpose(jnp.broadcast_to(term * valid, (LONG, 128)))[:8]
            put("term")
            g_pre = cot_column / (1.0 + jnp.exp(-pre))
            s.vec0[3:4, :] = column_sum(g_pre * mixed)
            s.vec0[4:5, :] = jnp.broadcast_to(column_sum(g_pre), (1, wide))
            copies.wait("left", "right")
            return s.cot[...].astype(F32) + g_pre * head

        def first_feed():
            for c in range(chunks):
                feed_loads(c)

        def next_loads():
            if not do_feed:
                product_starts()

        def after_feed():
            if do_attn:
                attn_loads()
                late_loads()
            else:
                product_starts()

        def norm_phase():
            if role == 1:
                grad = head_phase()
            else:
                copies.wait("left")
                grad = s.cot[...].astype(F32)
            copies.wait("r_xh2", "r_st")
            next_loads()
            xhat = s.xh2[...].astype(F32)
            s.vec0[0:1, :] = column_sum(grad * xhat)
            s.vec0[1:2, :] = column_sum(grad)
            dr2 = norm_back(grad, xhat, s.st[:, 64:65], i.g2[...].astype(F32))
            s.dr2[...] = dr2
            s.ddown[...] = dr2.astype(BF)
            put("ddown")
            s.vec0[2:3, :] = column_sum(s.ddown[...])
            put("vec0")

        def feed_phase():
            copies.wait(*[f"{n}{c}" for n in ("down", "dg", "up") for c in range(chunks)])
            after_feed()
            for c in range(chunks):
                cols = lane_block(c, chunk)
                dact = nt(s.ddown[...], s.down[cols, :])
                dlift = (dact * s.dg[:, cols].astype(F32)).astype(BF)
                s.dlift[:, cols] = dlift
                s.vec1[3 + c : 4 + c, :] = column_sum(dlift)
                part = nt(dlift, s.up[:, cols])
                s.acc[...] = part if c == 0 else s.acc[...] + part
                copies.start(f"dlift{c}", s.dlift.at[:, cols], o.dlift.at[slab, :, cols])
            copies.wait("r_xh1")
            dnormed = s.dr2[...] + s.acc[...]
            xhat = s.xh1[...].astype(F32)
            s.vec1[0:1, :] = column_sum(dnormed * xhat)
            s.vec1[1:2, :] = column_sum(dnormed)
            dr1 = norm_back(dnormed, xhat, s.st[:, 0:1], i.g1[...].astype(F32))
            s.dr1[...] = dr1
            s.dbranch[...] = dr1.astype(BF)
            put("dbranch")
            s.vec1[2:3, :] = column_sum(s.dbranch[...])
            put("vec1")

        def attn_phase():
            copies.wait("wo")
            s.datt[...] = nt(s.dbranch[...], s.wo[...]).astype(BF)
            copies.wait("r_rinv", "r_full", "r_v", "r_k", "r_q")
            if do_feed:
                for pair in range(PAIRS):
                    probs_in(pair).wait()

            def pair_step(pair, carry):
                if not do_feed:
                    probs_in(pair).wait()
                cols = lane_block(pair, PAIR)
                qp, kp, vp = s.q[:, cols], s.k[:, cols], s.v[:, cols]
                scaled = (s.datt[:, cols].astype(F32) * s.rinv[:, cols]).astype(BF)
                joint = scaled.astype(F32) * s.full[:, cols]
                parts = []
                for j in range(2):
                    here = in_half(j)
                    own = jnp.where(here, scaled, jnp.zeros_like(scaled))
                    delta = jnp.sum(jnp.where(here, joint, 0.0), axis=1, keepdims=True)
                    raised = s.p[2 * pair + j]
                    dscores = (raised.astype(F32) * (nt(own, vp) - delta)).astype(BF)
                    parts.append((nn(dscores, kp), tn(dscores, qp), tn(raised, scaled)))
                low = in_half(0)
                dq, dk, dv = (jnp.where(low, a, b) for a, b in zip(*parts))
                s.dqkv[:, cols] = (dq.astype(BF).astype(F32) * FACTOR).astype(BF)
                s.dqkv[:, lane_block(pair + PAIRS, PAIR)] = (dk * LN2).astype(BF)
                s.dqkv[:, lane_block(pair + 2 * PAIRS, PAIR)] = dv.astype(BF)
                return carry

            lax.fori_loop(0, PAIRS, pair_step, 0, unroll=3)
            put("dqkv")
            total = s.dr1[...]
            for n, name in enumerate(("wq", "wk", "wv")):
                copies.wait(name)
                total = total + nt(s.dqkv[:, lane_block(n, wide)], getattr(s, name)[...])
            s.dh[...] = total.astype(BF)
            copies.start("sent", s.dh if role == 1 else s.dh.at[:, pl.ds(half, half)], o.sent)
            put("dh")
            s.vec2[0:1, :] = column_sum(s.dqkv[:, lane_block(0, wide)])
            s.vec2[1:2, :] = column_sum(s.dqkv[:, lane_block(2, wide)])
            put("vec2")

        products_in = []
        for left, right in products:
            wide_left, wide_right = getattr(s, "w_" + left), getattr(s, right)
            setattr(s, "all_" + right, wide_right)
            setattr(s, right, wide_right.at[pl.ds(slab * LONG, LONG)])
            for t in range(count):
                at = pl.ds(t * LONG, LONG)
                pieces = [(getattr(i, "w_" + left), wide_left)]
                pieces += [(getattr(o, right), wide_right)] if t != slab else []
                for whole, part in pieces:
                    products_in.append(copies.make("in", whole.at[t], part.at[at]))
        copies.named.pop("in", None)

        def product_starts():
            for copy in products_in:
                copy.start()

        def product_phase():
            made_here = [
                copies.make("m" + right, getattr(o, right).at[slab], getattr(s, right))
                for _, right in products
            ]
            for _, right in products:
                copies.named.pop("m" + right)

            def fetch():
                for copy in made_here:
                    copy.start()
                for copy in made_here:
                    copy.wait()

            pl.when(i.section[0] != role)(fetch)
            for copy in products_in:
                copy.wait()
            step, base = wide, 0
            for left, right in products:
                whole_left, whole_right = getattr(s, "w_" + left), getattr(s, "all_" + right)
                width = whole_right.shape[1]
                for m in range(0, depth, step):
                    for n in range(0, width, step):
                        part = tn(
                            whole_left[:, m : m + step], whole_right[:, n : n + step]
                        ).astype(BF)
                        cols = pl.ds(base + n, step)
                        if not by_parts:
                            s.grad[m : m + step, cols] = part
                            continue
                        for j in range(m // share, (m + step) // share):
                            other_core = jnp.where(i.core[0] == j % 2, 0, 1)
                            at = j * share - m
                            spot = (j // 2) % 2 * 4 + j // 4
                            s.grad[other_core, spot, :, cols] = part[at : at + share]
                    if not by_parts:
                        continue
                if by_parts:
                    cols = pl.ds(base, width)
                    copies.start("keep" + left, s.grad.at[0, :, :, cols], o.keep.at[:, :, cols])
                    copies.start("send" + left, s.grad.at[1, :, :, cols], o.send.at[:, :, cols])
                base += width
            if not by_parts:
                copies.start("grad", s.grad, o.grad)
            copies.wait_all()

        def run():
            if do_norm:
                norm_loads()
            if do_norm and do_feed:
                first_feed()
            if do_feed and not do_norm:
                get("st")
            for n in links:
                far_ref = getattr(i, "l_" + n)
                copies.start(
                    "l_" + n, far_ref if n in ("dr1", "dr2") else far_ref.at[slab], getattr(s, n)
                )
            if do_norm:
                norm_phase()
            elif do_feed:
                first_feed()
            elif do_attn:
                attn_loads()
                late_loads()
            copies.wait(*["l_" + n for n in links])
            if do_feed:
                if not do_norm:
                    copies.wait("r_st")
                feed_phase()
            if do_attn:
                if not do_feed:
                    product_starts()
                attn_phase()
            for n in loose:
                if n in ("dr1", "dr2"):
                    copies.start("o" + n, getattr(s, n), getattr(o, n))
            copies.wait_all()

        pl.when(i.section[0] == role)(run)
        if products:
            pl.when(i.section[0] != role)(product_starts)
            product_phase()

    local = {}
    if do_norm:
        names = ("head_weight", "weight_cot", "g2") if role == 1 else ("g2",)
        local.update({n: vectors[n] for n in names})
    if do_feed:
        local.update(g1=vectors["g1"])
    result = call(
        "backward_" + "_".join(phases), body, scalars, local, far, outs, scratch, 88,
        6_000_000_000 * len(phases), {n: made[n] for n in stacks} if made else None,
    )
    return dict(made or {}, **{n: result[n] for n in stacks}), {n: result[n] for n in loose}


def pick(array_in, index, axis):
    return lax.dynamic_index_in_dim(array_in, index, axis, keepdims=False)


def cut(array_in, start, size):
    return lax.dynamic_slice_in_dim(array_in, start, size, 0)


def added(*pieces):
    total = pieces[0].astype(F32)
    for piece in pieces[1:]:
        total = total + piece.astype(F32)
    return total


def routed(block, pairs):
    return lax.ppermute(block, "dp", pairs)


def swap_bit(block, bit):
    return routed(block, [(i, i ^ bit) for i in range(lax.axis_size("dp"))])


def behind(array_in, *others):
    return lax.optimization_barrier((array_in,) + others)[0]


def join(mine, got, start, cost):
    def kernel(start_ref, mine_ref, got_ref, sum_ref, send_ref):
        for j in range(4):
            sum_ref[j] = added(mine_ref[j], got_ref[j]).astype(BF)
        for j in range(3):
            send_ref[j] = sum_ref[start_ref[0] + j]

    local = pl.BlockSpec(memory_space=pltpu.VMEM)
    return pl.pallas_call(
        kernel,
        out_shape=[
            jax.ShapeDtypeStruct(mine.shape, BF),
            jax.ShapeDtypeStruct((3,) + mine.shape[1:], BF),
        ],
        in_specs=[pl.BlockSpec(memory_space=pltpu.SMEM), local, local],
        out_specs=[local, local],
        compiler_params=pltpu.CompilerParams(vmem_limit_bytes=32 << 20),
        cost_estimate=pl.CostEstimate(flops=cost, bytes_accessed=8_000_000, transcendentals=0),
        name="join_quarters",
    )(start, mine, got)


class ShardSum:
    def __init__(self, made):
        self.by_parts = "send" in made
        if not self.by_parts:
            self.grad = made["grad"]
            self.mark = (self.grad,)
            return
        me = lax.axis_index("dp")
        self.side, self.place = (me // 2) % 2, me // 4
        self.lower = self.place <= 1
        in_lines = lambda array: array.reshape((2, 4) + array.shape[1:])
        self.mine, self.got = in_lines(made["keep"]), swap_bit(in_lines(made["send"]), 1)
        self.mark = (made["send"],)

    def step(self, run, *before):
        if self.by_parts:
            if before:
                self.got = behind(self.got, *before)
            self.mark = (run(),)
        return self

    def to_line(self, *before):
        def run():
            mine, got, side = self.mine, self.got, self.side
            send = added(pick(mine, 1 - side, 0), pick(got, 1 - side, 0)).astype(BF)
            self.keep = added(pick(mine, side, 0), pick(got, side, 0)).astype(BF)
            self.got = swap_bit(send, 2)
            return send

        return self.step(run, *before)

    def inwards(self, *before, cost=1_000_000_000):
        def run():
            start = jnp.where(self.place == 0, 1, 0).astype(jnp.int32)[None]
            self.blocks, send = join(self.keep, self.got, start, cost)
            row = range(4)
            self.got = routed(send, [(j, j + 4) for j in row] + [(j + 12, j + 8) for j in row])
            return send

        return self.step(run, *before)

    def across(self, *before):
        def run():
            lower, row = self.lower, range(4)
            self.ends = self.got
            send = added(
                cut(self.blocks, jnp.where(lower, 2, 0), 2),
                cut(self.ends, jnp.where(lower, 1, 0), 2),
            ).astype(BF)
            self.got = routed(send, [(j + 4, j + 8) for j in row] + [(j + 8, j + 4) for j in row])
            return send

        return self.step(run, *before)

    def outwards(self, *before):
        def run():
            lower, row = self.lower, range(4)
            self.middle = self.got
            send = added(
                pick(self.blocks, jnp.where(lower, 0, 3), 0),
                pick(self.middle, jnp.where(lower, 0, 1), 0),
            ).astype(BF)
            self.got = routed(send, [(j + 4, j) for j in row] + [(j + 8, j + 12) for j in row])
            return send

        return self.step(run, *before)

    def last(self, *before):
        if not self.by_parts:
            return lax.psum_scatter(
                self.grad.astype(F32), "dp", scatter_dimension=0, tiled=True
            )
        got = behind(self.got, *before) if before else self.got
        total = added(
            pick(self.blocks, self.place, 0),
            pick(self.ends, jnp.where(self.lower, 0, 2), 0),
            pick(self.middle, jnp.where(self.lower, 1, 0), 0),
            got,
        )
        self.mark = (total,)
        return total


def body(
    tokens,
    out_cot,
    weight_cot,
    plan,
    lengths,
    q_weight,
    k_weight,
    v_weight,
    o_weight,
    q_bias,
    v_bias,
    o_bias,
    norm1_gain,
    norm1_bias,
    up_weight,
    up_bias,
    down_weight,
    down_bias,
    norm2_gain,
    norm2_bias,
    head_weight,
    head_bias,
):
    my_section = lax.axis_index("pipe")
    is_first = my_section == 0
    section = my_section.astype(jnp.int32)[None]
    row_count, half = tokens.shape
    wide, deep = up_weight.shape[1:]
    count = row_count // LONG
    dp_count = lax.axis_size("dp")
    share = wide // dp_count
    to_next, to_back = [(0, 1)], [(1, 0)]
    slab_of = lambda array, j: array[j * LONG : (j + 1) * LONG]
    over = lambda array, way: lax.ppermute(array, "pipe", way)
    token_other = [over(slab_of(tokens, 0), to_back)]
    for j in range(1, count):
        token_other.append(over(behind(slab_of(tokens, j), token_other[-1]), to_back))
    cot_other = over(out_cot, to_next)
    weights = dict(
        wq=q_weight, wk=k_weight, wv=v_weight, wo=o_weight, up=up_weight, down=down_weight
    )
    vectors = dict(
        qb=q_bias, vb=v_bias, ob=o_bias, g1=norm1_gain, b1=norm1_bias, upb=up_bias,
        downb=down_bias, g2=norm2_gain, b2=norm2_bias,
    )
    kept, recv = None, []
    for j in range(count):
        kept, sent = forward_slab(
            0, j, count, section, plan, lengths, tokens, token_other[j], None, weights, vectors,
            kept, [cot_other] if j else [],
        )
        recv.append(over(sent, to_next))
    mixed_got = []
    for j in range(count):
        kept, sent = forward_slab(
            1, j, count, section, plan, lengths, None, None, recv[j], weights, vectors, kept, []
        )
        mixed_got.append(over(sent, to_back))
    scalars = dict(section=section, plan=plan, lengths=lengths, head_bias=head_bias)
    vectors = dict(
        g1=norm1_gain, g2=norm2_gain, head_weight=head_weight[None],
        weight_cot=weight_cot.reshape(count, 1, LONG),
    )
    full = ("norm", "feed", "attn")
    made, recv = None, [None] * count
    for j in reversed(range(count)):
        made, loose = backward_slab(
            1, j, count, full, scalars, vectors, dict(own=out_cot, other=cot_other), weights, kept,
            {}, made, [mixed_got[count - 1 - j]],
        )
        recv[j] = over(loose["sent"], to_back)
    token_got = [None] * count
    for j in reversed(range(1, count)):
        made, loose = backward_slab(
            0, j, count, full, scalars, vectors, dict(recv=recv[j]), weights, kept, {}, made
        )
        token_got[j] = loose["sent"]
    head_sums = jnp.sum(made["vec0"][:, 3:5], axis=0)
    term = made["term"][:, 0].reshape(row_count)
    early = jnp.concatenate([term, head_sums[0], head_sums[1, :1]])
    scalars["core"] = (lax.axis_index("dp") % 2).astype(jnp.int32)[None]
    last = functools.partial(backward_slab, 0, 0, count)
    made, loose = last(
        ("norm",), scalars, vectors, dict(recv=recv[0]), weights, kept, {}, made, [],
        dp_count,
    )
    down_sum = ShardSum(loose).to_line()
    made, loose = last(
        ("feed",), scalars, vectors, {}, weights, kept, dict(loose, ddown=made["ddown"]), made,
        down_sum.mark, dp_count,
    )
    feed_sum = ShardSum(loose)
    down_sum.inwards(*feed_sum.mark, cost=60_000_000_000)
    feed_sum.to_line(*down_sum.mark)
    made, loose = last(
        ("attn",), scalars, vectors, {}, weights, kept, dict(loose, dbranch=made["dbranch"]), made,
        feed_sum.mark + down_sum.mark, dp_count,
    )
    qkv_sum = ShardSum(loose)
    down_sum.across(*qkv_sum.mark)
    feed_sum.inwards(*down_sum.mark, cost=60_000_000_000)
    qkv_sum.to_line(*feed_sum.mark)
    down_sum.outwards(*qkv_sum.mark)
    feed_sum.across(*down_sum.mark)
    early_got = over(behind(early, *down_sum.mark), to_back)
    token_got[0] = loose["sent"]
    token_got = [over(behind(array, *down_sum.mark), to_next) for array in token_got]
    qkv_sum.inwards(*feed_sum.mark, early_got)
    early = jnp.where(is_first, early_got, early)
    sums0, sums1, sums2 = (
        jnp.sum(behind(made[n], *qkv_sum.mark), axis=0) for n in ("vec0", "vec1", "vec2")
    )
    lines = jnp.concatenate(
        [sums2[:2], sums1[2:3], sums1[:2], sums0[2:3], sums0[:2], early[None, row_count:-1]]
    )
    flat = jnp.concatenate(
        [
            lines.reshape(9, dp_count, share).transpose(1, 0, 2).reshape(dp_count, -1),
            sums1[3 : 3 + deep // wide].reshape(dp_count, -1),
            jnp.broadcast_to(early[None, -1:], (dp_count, 1)),
        ],
        axis=1,
    )
    if qkv_sum.by_parts:
        flat = flat + swap_bit(flat, 1)
        flat = flat + swap_bit(flat, 2)
        near, far, farther = (swap_bit(flat, bits) for bits in (4, 8, 12))
        qkv_sum.across(flat)
        feed_sum.outwards(*qkv_sum.mark)
        qkv_sum.outwards(*feed_sum.mark)
        near = behind(near, *qkv_sum.mark)
        flat = pick((flat + near) + (far + farther), lax.axis_index("dp"), 0)
        down_grad = down_sum.last(*qkv_sum.mark)
        feed_grad = feed_sum.last(*qkv_sum.mark)
    else:
        flat = lax.psum_scatter(flat, "dp", scatter_dimension=0, tiled=True)[0]
        down_grad, feed_grad = down_sum.last(), feed_sum.last()
    qkv_grad = qkv_sum.last()
    up_grad, o_grad = feed_grad[:, :deep], feed_grad[:, deep:]
    at = lambda j: flat[j * share : (j + 1) * share]
    out_rows = kept["out"].reshape(row_count, wide)
    grad_rows = made["dh"].reshape(row_count, wide)
    others = jnp.concatenate(mixed_got), jnp.concatenate(token_got)
    others = [behind(array, *qkv_sum.mark) for array in others]
    mixed_out = jnp.where(is_first, others[0], out_rows[:, half:])
    tokens_grad = jnp.where(is_first, grad_rows[:, :half], others[1])
    return (
        mixed_out,
        early[:row_count],
        tokens_grad,
        qkv_grad[None, :, :wide],
        qkv_grad[None, :, wide : 2 * wide],
        qkv_grad[None, :, 2 * wide :],
        o_grad[None],
        at(0)[None],
        at(1)[None],
        at(2)[None],
        at(3)[None],
        at(4)[None],
        up_grad[None],
        flat[None, 9 * share : 9 * share + deep // dp_count],
        down_grad[None],
        at(5)[None],
        at(6)[None],
        at(7)[None],
        at(8),
        flat[-1:],
    )


def solution(mesh):
    rows, stack, flat = P("dp", "pipe"), P("pipe", None, None), P("pipe", None)
    in_specs = (
        (rows, rows, P("dp"), P("dp"), P("dp", None))
        + (stack,) * 4
        + (flat,) * 5
        + (stack, flat, stack, flat, flat, flat, P(), P())
    )
    shard, line = P("pipe", "dp", None), P("pipe", "dp")
    out_specs = (
        (rows, P("dp"), rows)
        + (shard,) * 4
        + (line,) * 5
        + (shard, line, shard, line, line, line, P("dp"), P())
    )
    return jax.shard_map(body, mesh=mesh, in_specs=in_specs, out_specs=out_specs, check_vma=False)
```

```python
import functools
from types import SimpleNamespace

import jax
import jax.numpy as jnp
from jax import lax
from jax.experimental import pallas as pl
from jax.experimental.pallas import tpu as pltpu
from jax.sharding import PartitionSpec as P

HEADS = 12
HEAD = 64
PAIR = 2 * HEAD
PAIRS = HEADS // 2
SHORT = 128
LONG = 512
EPSILON = 1e-06
MASKED = -1e30
FACTOR = HEAD**-0.5
LOG2E = 1.4426950408889634
LN2 = 0.6931471805599453
BF = jnp.bfloat16
F32 = jnp.float32
VMEM_BYTES = 58 << 20


def product(dims, left_side, right_side):
    return lax.dot_general(left_side, right_side, (dims, ((), ())), preferred_element_type=F32)


nn = functools.partial(product, ((1,), (0,)))
nt = functools.partial(product, ((1,), (1,)))
tn = functools.partial(product, ((0,), (0,)))


def segment_limits(plan, lengths, slab, position):
    is_long = plan[slab] == 1
    parts = [lengths[slab, j] for j in range(LONG // SHORT)]
    slot = position // SHORT
    own = jnp.full(position.shape, parts[-1], jnp.int32)
    for j in range(len(parts) - 1):
        own = jnp.where(slot == j, parts[j], own)
    limit = jnp.where(is_long, sum(parts), own + slot * SHORT)
    return jnp.where(is_long, 0, slot), position < limit


def row_mean(rows_in):
    return jnp.mean(rows_in, axis=1, keepdims=True)


def column_sum(rows_in):
    return jnp.sum(rows_in.astype(F32), axis=0, keepdims=True)


def in_half(j):
    lane = lax.broadcasted_iota(jnp.int32, (LONG, PAIR), 1)
    return (lane < HEAD) if j == 0 else (lane >= HEAD)


def lane_block(index, width):
    start = index * width
    return pl.ds(start if isinstance(index, int) else pl.multiple_of(start, width), width)


class Copies:
    def __init__(self, sems):
        self.sems, self.used, self.named = sems, 0, {}

    def make(self, name, src, dst):
        copy = pltpu.make_async_copy(src, dst, self.sems.at[self.used])
        self.used += 1
        self.named[name] = copy
        return copy

    def start(self, name, src, dst):
        self.make(name, src, dst).start()

    def wait(self, *names):
        for name in names:
            self.named.pop(name).wait()

    def wait_all(self):
        self.wait(*list(self.named))


def call(name, body, scalars, local, far, outs, scratch, sems, cost, kept=None):
    kept = kept or {}
    names = list(scalars) + list(local) + list(far)
    arrays = list(scalars.values()) + list(local.values()) + list(far.values())
    specs = [pl.BlockSpec(memory_space=pltpu.SMEM)] * len(scalars)
    specs += [pl.BlockSpec(memory_space=pltpu.VMEM)] * len(local)
    specs += [pl.BlockSpec(memory_space=pl.ANY)] * (len(far) + len(kept))
    aliases = {}
    for key, array in kept.items():
        aliases[len(arrays)] = list(outs).index(key)
        arrays.append(array)
    skip = len(kept)

    def kernel(*refs):
        refs = list(refs)
        given, rest = refs[: len(names)], refs[len(names) + skip :]
        n = len(outs)
        body(
            SimpleNamespace(**dict(zip(names, given))),
            SimpleNamespace(**dict(zip(outs, rest[:n]))),
            SimpleNamespace(**dict(zip(scratch, rest[n : n + len(scratch)]))),
            Copies(rest[-1]),
        )

    made = pl.pallas_call(
        kernel,
        out_shape=[jax.ShapeDtypeStruct(d, k) for d, k in outs.values()],
        in_specs=specs,
        out_specs=[pl.BlockSpec(memory_space=pl.ANY)] * len(outs),
        scratch_shapes=[pltpu.VMEM(d, k) for d, k in scratch.values()]
        + [pltpu.SemaphoreType.DMA((sems,))],
        input_output_aliases=aliases,
        compiler_params=pltpu.CompilerParams(vmem_limit_bytes=VMEM_BYTES),
        cost_estimate=pl.CostEstimate(flops=cost, bytes_accessed=30_000_000, transcendentals=0),
        name=name,
    )(*arrays)
    return dict(zip(outs, made))


def forward_slab(
    role, slab, count, section, plan, lengths, own, other, recv, weights, vectors, kept, after
):
    wide, deep = weights["wq"].shape[1], weights["up"].shape[2]
    half = wide // 2
    rows = (LONG, wide)
    stack = {
        "h": (rows, BF), "q": (rows, BF), "k": (rows, BF), "v": (rows, BF),
        "p": ((HEADS, LONG, LONG), BF), "att": (rows, BF), "full": (rows, F32),
        "rinv": (rows, F32), "xh1": (rows, BF), "nl": (rows, BF), "act": ((LONG, deep), BF),
        "dg": ((LONG, deep), BF), "xh2": (rows, BF), "st": ((LONG, 128), F32), "out": (rows, BF),
    }
    outs = {n: ((count,) + d, k) for n, (d, k) in stack.items()}
    outs["sent"] = (rows if role == 0 else (LONG, half), BF)
    scratch = dict(stack)
    scratch.update({n: (w.shape[1:], BF) for n, w in weights.items()})
    scratch.update({
        "normed": (rows, F32), "acc": (rows, F32), "qfeat": ((LONG, PAIR), BF),
        "kfeat": ((LONG, PAIR), BF),
    })
    far = dict(weights)
    far.update(dict(own=own, other=other) if role == 0 else dict(recv=recv))
    far.update({f"after{n}": array for n, array in enumerate(after)})
    chunk = wide
    chunks = deep // chunk

    def body(i, o, s, copies):
        def run():
            if role == 0:
                mine = pl.ds(slab * LONG, LONG)
                copies.start("left", i.own.at[mine], s.h.at[:, pl.ds(0, half)])
                copies.start("right", i.other, s.h.at[:, pl.ds(half, half)])
            else:
                copies.start("left", i.recv, s.h)
            for n in ("wq", "wk", "wv"):
                copies.start(n, getattr(i, n).at[0], getattr(s, n))

            def rest_loads():
                copies.start("wo", i.wo.at[0], s.wo)
                for c in range(chunks):
                    cols = lane_block(c, chunk)
                    copies.start(f"up{c}", i.up.at[0, :, cols], s.up.at[:, cols])
                    copies.start(f"down{c}", i.down.at[0, cols, :], s.down.at[cols, :])

            def store(name):
                copies.start("o" + name, getattr(s, name), getattr(o, name).at[slab])

            lane = lax.broadcasted_iota(jnp.int32, (LONG, PAIR), 1) % HEAD
            at = lax.broadcasted_iota(jnp.int32, (LONG, PAIR), 0)
            segment, valid = segment_limits(i.plan, i.lengths, slab, at)
            s.qfeat[...] = jnp.where(segment == lane, 1.0, 0.0).astype(BF)
            closed = (lane < LONG // SHORT) & ((segment != lane) | jnp.logical_not(valid))
            s.kfeat[...] = jnp.where(closed, MASKED, 0.0).astype(BF)
            copies.wait(*(["left", "right"] if role == 0 else ["left"]))
            hidden = s.h[...]
            copies.wait("wq", "wk", "wv")
            rest_loads()
            queries = nn(hidden, s.wq[...]) + i.qb[...].astype(F32)
            s.q[...] = (queries * (FACTOR * LOG2E)).astype(BF)
            s.k[...] = nn(hidden, s.wk[...]).astype(BF)
            store("h")
            store("q")
            store("k")
            s.v[...] = (nn(hidden, s.wv[...]) + i.vb[...].astype(F32)).astype(BF)
            store("v")
            base = copies.used
            copies.used += PAIRS

            def probs_out(pair):
                two = pl.ds(2 * pair, 2)
                return pltpu.make_async_copy(
                    s.p.at[two], o.p.at[slab, two], copies.sems.at[base + pair]
                )

            def pair_step(pair, carry):
                cols = lane_block(pair, PAIR)
                qp, kp, vp = s.q[:, cols], s.k[:, cols], s.v[:, cols]
                sides = []
                for j in range(2):
                    here = in_half(j)
                    scores = nt(
                        jnp.where(here, qp, s.qfeat[...]), jnp.where(here, kp, s.kfeat[...])
                    )
                    top = jnp.max(scores, axis=1, keepdims=True)
                    raised = jnp.exp2(scores - top).astype(BF)
                    s.p[2 * pair + j] = raised
                    sides.append(nn(raised, jnp.where(here, vp, jnp.ones_like(vp))))
                low = in_half(0)
                rinv = 1.0 / pltpu.roll(jnp.where(low, sides[1], sides[0]), HEAD, 1)
                mix = jnp.where(low, sides[0], sides[1]) * rinv
                s.full[:, cols] = mix
                s.rinv[:, cols] = rinv
                s.att[:, cols] = mix.astype(BF)
                probs_out(pair).start()
                return carry

            lax.fori_loop(0, PAIRS, pair_step, 0, unroll=3)
            for n in ("att", "full", "rinv"):
                store(n)
            copies.wait("wo")
            res = hidden.astype(F32) + (nn(s.att[...], s.wo[...]) + i.ob[...].astype(F32))
            centre = res - row_mean(res)
            rstd1 = lax.rsqrt(row_mean(centre * centre) + EPSILON)
            xhat = centre * rstd1
            normed = xhat * i.g1[...].astype(F32) + i.b1[...].astype(F32)
            s.xh1[...] = xhat.astype(BF)
            s.nl[...] = normed.astype(BF)
            s.normed[...] = normed
            store("xh1")
            store("nl")
            copies.wait(*[f"{n}{c}" for n in ("up", "down") for c in range(chunks)])
            for c in range(chunks):
                cols = lane_block(c, chunk)
                lifted = nn(s.nl[...], s.up[:, cols]) + i.upb[:, cols].astype(F32)
                cdf = 0.5 + 0.5 * lax.erf(lifted * 0.7071067811865476)
                act = (lifted * cdf).astype(BF)
                dens = jnp.exp2(lifted * lifted * (-0.5 * LOG2E)) * 0.3989422804014327
                s.act[:, cols] = act
                s.dg[:, cols] = (cdf + lifted * dens).astype(BF)
                part = nn(act, s.down[cols, :])
                s.acc[...] = part if c == 0 else s.acc[...] + part
                copies.start(f"act{c}", s.act.at[:, cols], o.act.at[slab, :, cols])
                copies.start(f"dg{c}", s.dg.at[:, cols], o.dg.at[slab, :, cols])
            res = s.normed[...] + s.acc[...] + i.downb[...].astype(F32)
            centre = res - row_mean(res)
            rstd2 = lax.rsqrt(row_mean(centre * centre) + EPSILON)
            xhat = centre * rstd2
            s.out[...] = (xhat * i.g2[...].astype(F32) + i.b2[...].astype(F32)).astype(BF)
            copies.start("sent", s.out if role == 0 else s.out.at[:, pl.ds(0, half)], o.sent)
            if role == 1:
                store("out")
            s.xh2[...] = xhat.astype(BF)
            store("xh2")
            side = lax.broadcasted_iota(jnp.int32, (LONG, 128), 1)
            s.st[...] = jnp.where(side < 64, rstd1, rstd2)
            store("st")
            for pair in range(PAIRS):
                probs_out(pair).wait()
            copies.wait_all()

        pl.when(i.section[0] == role)(run)

    made = call(
        "forward_layer", body, dict(section=section, plan=plan, lengths=lengths), vectors, far,
        outs, scratch, 64, 16_000_000_000, kept,
    )
    sent = made.pop("sent")
    return made, sent


def norm_back(grad, xhat, rstd, gain):
    scaled = grad * gain
    return rstd * (scaled - row_mean(scaled) - xhat * row_mean(scaled * xhat))


def backward_slab(
    role, slab, count, phases, scalars, vectors, cots, weights, kept, passed, made, after=(),
    dp_count=0,
):
    do_norm, do_feed, do_attn = (n in phases for n in ("norm", "feed", "attn"))
    wide, deep = kept["h"].shape[2], kept["act"].shape[2]
    rows = (LONG, wide)
    half = wide // 2
    chunk = wide
    chunks = deep // chunk
    stacks, loose = {}, {}
    uses, needs, links = [], [], []
    if do_norm:
        stacks.update(ddown=(rows, BF), vec0=((8, wide), F32))
        uses += ["xh2", "st"]
        if role == 1:
            stacks.update(term=((8, LONG), F32))
            uses += ["out"]
    if do_feed:
        stacks.update(dlift=((LONG, deep), BF), dbranch=(rows, BF), vec1=((8, wide), F32))
        uses += ["dg", "xh1"] + ([] if do_norm else ["st"])
        needs += ["down", "up"]
    if do_attn:
        stacks.update(dqkv=((LONG, 3 * wide), BF), vec2=((8, wide), F32), dh=(rows, BF))
        uses += ["full", "rinv", "q", "k", "v", "p"]
        needs += ["wo", "wq", "wk", "wv"]
        loose.update(sent=(rows if role == 1 else (LONG, half), BF))
    if do_norm and not do_feed:
        loose.update(dr2=(rows, F32))
    if do_feed and not do_attn:
        loose.update(dr1=(rows, F32))
    if do_feed and not do_norm:
        links += ["dr2", "ddown"]
    if do_attn and not do_feed:
        links += ["dr1", "dbranch"]
    products, depth = [], 0
    by_parts = dp_count == 16
    if dp_count:
        products += [("act", "ddown")] if do_norm else []
        products += [("nl", "dlift"), ("att", "dbranch")] if do_feed else []
        products += [("h", "dqkv")] if do_attn else []
        depth = kept[products[0][0]].shape[2]
    far = {"r_" + n: kept[n] for n in uses}
    far.update({"w_" + left: kept[left] for left, right in products})
    far.update({n: weights[n] for n in needs})
    far.update({"l_" + n: passed[n] for n in links})
    if do_norm:
        far.update(cots)
    far.update({f"after{n}": array for n, array in enumerate(after)})
    outs = {n: ((count,) + d, k) for n, (d, k) in stacks.items()}
    outs.update(loose)
    scratch = {n: (kept[n].shape[1:], kept[n].dtype) for n in uses}
    scratch.update({n: (weights[n].shape[1:], BF) for n in needs})
    scratch.update(stacks)
    scratch.update(dr2=(rows, F32), dr1=(rows, F32))
    if do_norm:
        scratch.update(cot=(rows, BF))
    if do_feed:
        scratch.update(acc=(rows, F32), ddown=(rows, BF))
    if do_attn:
        scratch.update(datt=(rows, BF), dbranch=(rows, BF))
    if products:
        across = sum(stacks[right][0][1] for left, right in products)
        share = depth // dp_count
        if by_parts:
            scratch.update(grad=((2, dp_count // 2, share, across), BF))
            loose.update(send=((dp_count // 2, share, across), BF))
            loose.update(keep=((dp_count // 2, share, across), BF))
        else:
            scratch.update(grad=((depth, across), BF))
            loose.update(grad=((depth, across), BF))
        outs.update(loose)
        for left, right in products:
            scratch["w_" + left] = ((count * LONG, depth), BF)
            scratch[right] = ((count * LONG, stacks[right][0][1]), BF)

    def body(i, o, s, copies):
        probs_sems = copies.sems.at[pl.ds(0, PAIRS)]
        copies.used = PAIRS

        def get(name):
            copies.start("r_" + name, getattr(i, "r_" + name).at[slab], getattr(s, name))

        def get_weight(name):
            copies.start(name, getattr(i, name).at[0], getattr(s, name))

        def put(name):
            copies.start("o" + name, getattr(s, name), getattr(o, name).at[slab])

        def norm_loads():
            if role == 1:
                get("out")
                mine = pl.ds(slab * LONG, LONG)
                copies.start("left", i.other.at[mine], s.cot.at[:, pl.ds(0, half)])
                copies.start("right", i.own.at[mine], s.cot.at[:, pl.ds(half, half)])
            else:
                copies.start("left", i.recv, s.cot)
            get("xh2")
            get("st")

        def feed_loads(c):
            cols = lane_block(c, chunk)
            copies.start(f"down{c}", i.down.at[0, cols, :], s.down.at[cols, :])
            copies.start(f"dg{c}", i.r_dg.at[slab, :, cols], s.dg.at[:, cols])
            copies.start(f"up{c}", i.up.at[0, :, cols], s.up.at[:, cols])
            if c == chunks - 1:
                get("xh1")

        def attn_loads():
            get_weight("wo")
            for n in ("rinv", "full", "v", "k", "q"):
                get(n)

        def probs_in(pair):
            two = pl.ds(2 * pair, 2)
            return pltpu.make_async_copy(i.r_p.at[slab, two], s.p.at[two], probs_sems.at[pair])

        def late_loads():
            for pair in range(PAIRS):
                probs_in(pair).start()
            for n in ("wq", "wk", "wv"):
                get_weight(n)

        def head_phase():
            position = lax.broadcasted_iota(jnp.int32, (LONG, 1), 0)
            valid = segment_limits(i.plan, i.lengths, slab, position)[1]
            valid = jnp.where(valid, 1.0, 0.0)
            cot_row = jnp.broadcast_to(i.weight_cot[slab], (8, LONG))
            cot_column = jnp.transpose(cot_row)[:, :1] * valid
            copies.wait("r_out")
            mixed = s.out[...].astype(F32)
            head = i.head_weight[...].astype(F32)
            pre = jnp.sum(mixed * head, axis=1, keepdims=True) + i.head_bias[0]
            term = jnp.maximum(pre, 0.0) + jnp.log1p(jnp.exp(-jnp.abs(pre)))
            s.term[...] = jnp.transpose(jnp.broadcast_to(term * valid, (LONG, 128)))[:8]
            put("term")
            g_pre = cot_column / (1.0 + jnp.exp(-pre))
            s.vec0[3:4, :] = column_sum(g_pre * mixed)
            s.vec0[4:5, :] = jnp.broadcast_to(column_sum(g_pre), (1, wide))
            copies.wait("left", "right")
            return s.cot[...].astype(F32) + g_pre * head

        def first_feed():
            for c in range(chunks):
                feed_loads(c)

        def next_loads():
            if not do_feed:
                product_starts()

        def after_feed():
            if do_attn:
                attn_loads()
                late_loads()
            else:
                product_starts()

        def norm_phase():
            if role == 1:
                grad = head_phase()
            else:
                copies.wait("left")
                grad = s.cot[...].astype(F32)
            copies.wait("r_xh2", "r_st")
            next_loads()
            xhat = s.xh2[...].astype(F32)
            s.vec0[0:1, :] = column_sum(grad * xhat)
            s.vec0[1:2, :] = column_sum(grad)
            dr2 = norm_back(grad, xhat, s.st[:, 64:65], i.g2[...].astype(F32))
            s.dr2[...] = dr2
            s.ddown[...] = dr2.astype(BF)
            put("ddown")
            s.vec0[2:3, :] = column_sum(s.ddown[...])
            put("vec0")

        def feed_phase():
            copies.wait(*[f"{n}{c}" for n in ("down", "dg", "up") for c in range(chunks)])
            after_feed()
            for c in range(chunks):
                cols = lane_block(c, chunk)
                dact = nt(s.ddown[...], s.down[cols, :])
                dlift = (dact * s.dg[:, cols].astype(F32)).astype(BF)
                s.dlift[:, cols] = dlift
                s.vec1[3 + c : 4 + c, :] = column_sum(dlift)
                part = nt(dlift, s.up[:, cols])
                s.acc[...] = part if c == 0 else s.acc[...] + part
                copies.start(f"dlift{c}", s.dlift.at[:, cols], o.dlift.at[slab, :, cols])
            copies.wait("r_xh1")
            dnormed = s.dr2[...] + s.acc[...]
            xhat = s.xh1[...].astype(F32)
            s.vec1[0:1, :] = column_sum(dnormed * xhat)
            s.vec1[1:2, :] = column_sum(dnormed)
            dr1 = norm_back(dnormed, xhat, s.st[:, 0:1], i.g1[...].astype(F32))
            s.dr1[...] = dr1
            s.dbranch[...] = dr1.astype(BF)
            put("dbranch")
            s.vec1[2:3, :] = column_sum(s.dbranch[...])
            put("vec1")

        def attn_phase():
            copies.wait("wo")
            s.datt[...] = nt(s.dbranch[...], s.wo[...]).astype(BF)
            copies.wait("r_rinv", "r_full", "r_v", "r_k", "r_q")
            if do_feed:
                for pair in range(PAIRS):
                    probs_in(pair).wait()

            def pair_step(pair, carry):
                if not do_feed:
                    probs_in(pair).wait()
                cols = lane_block(pair, PAIR)
                qp, kp, vp = s.q[:, cols], s.k[:, cols], s.v[:, cols]
                scaled = (s.datt[:, cols].astype(F32) * s.rinv[:, cols]).astype(BF)
                joint = scaled.astype(F32) * s.full[:, cols]
                parts = []
                for j in range(2):
                    here = in_half(j)
                    own = jnp.where(here, scaled, jnp.zeros_like(scaled))
                    delta = jnp.sum(jnp.where(here, joint, 0.0), axis=1, keepdims=True)
                    raised = s.p[2 * pair + j]
                    dscores = (raised.astype(F32) * (nt(own, vp) - delta)).astype(BF)
                    parts.append((nn(dscores, kp), tn(dscores, qp), tn(raised, scaled)))
                low = in_half(0)
                dq, dk, dv = (jnp.where(low, a, b) for a, b in zip(*parts))
                s.dqkv[:, cols] = (dq.astype(BF).astype(F32) * FACTOR).astype(BF)
                s.dqkv[:, lane_block(pair + PAIRS, PAIR)] = (dk * LN2).astype(BF)
                s.dqkv[:, lane_block(pair + 2 * PAIRS, PAIR)] = dv.astype(BF)
                return carry

            lax.fori_loop(0, PAIRS, pair_step, 0, unroll=3)
            put("dqkv")
            total = s.dr1[...]
            for n, name in enumerate(("wq", "wk", "wv")):
                copies.wait(name)
                total = total + nt(s.dqkv[:, lane_block(n, wide)], getattr(s, name)[...])
            s.dh[...] = total.astype(BF)
            copies.start("sent", s.dh if role == 1 else s.dh.at[:, pl.ds(half, half)], o.sent)
            put("dh")
            s.vec2[0:1, :] = column_sum(s.dqkv[:, lane_block(0, wide)])
            s.vec2[1:2, :] = column_sum(s.dqkv[:, lane_block(2, wide)])
            put("vec2")

        products_in = []
        for left, right in products:
            wide_left, wide_right = getattr(s, "w_" + left), getattr(s, right)
            setattr(s, "all_" + right, wide_right)
            setattr(s, right, wide_right.at[pl.ds(slab * LONG, LONG)])
            for t in range(count):
                at = pl.ds(t * LONG, LONG)
                pieces = [(getattr(i, "w_" + left), wide_left)]
                pieces += [(getattr(o, right), wide_right)] if t != slab else []
                for whole, part in pieces:
                    products_in.append(copies.make("in", whole.at[t], part.at[at]))
        copies.named.pop("in", None)

        def product_starts():
            for copy in products_in:
                copy.start()

        def product_phase():
            made_here = [
                copies.make("m" + right, getattr(o, right).at[slab], getattr(s, right))
                for _, right in products
            ]
            for _, right in products:
                copies.named.pop("m" + right)

            def fetch():
                for copy in made_here:
                    copy.start()
                for copy in made_here:
                    copy.wait()

            pl.when(i.section[0] != role)(fetch)
            for copy in products_in:
                copy.wait()
            step, base = wide, 0
            for left, right in products:
                whole_left, whole_right = getattr(s, "w_" + left), getattr(s, "all_" + right)
                width = whole_right.shape[1]
                for m in range(0, depth, step):
                    for n in range(0, width, step):
                        part = tn(
                            whole_left[:, m : m + step], whole_right[:, n : n + step]
                        ).astype(BF)
                        cols = pl.ds(base + n, step)
                        if not by_parts:
                            s.grad[m : m + step, cols] = part
                            continue
                        for j in range(m // share, (m + step) // share):
                            other_core = jnp.where(i.core[0] == j % 2, 0, 1)
                            at = j * share - m
                            spot = (j // 2) % 2 * 4 + j // 4
                            s.grad[other_core, spot, :, cols] = part[at : at + share]
                    if not by_parts:
                        continue
                if by_parts:
                    cols = pl.ds(base, width)
                    copies.start("keep" + left, s.grad.at[0, :, :, cols], o.keep.at[:, :, cols])
                    copies.start("send" + left, s.grad.at[1, :, :, cols], o.send.at[:, :, cols])
                base += width
            if not by_parts:
                copies.start("grad", s.grad, o.grad)
            copies.wait_all()

        def run():
            if do_norm:
                norm_loads()
            if do_norm and do_feed:
                first_feed()
            if do_feed and not do_norm:
                get("st")
            for n in links:
                far_ref = getattr(i, "l_" + n)
                copies.start(
                    "l_" + n, far_ref if n in ("dr1", "dr2") else far_ref.at[slab], getattr(s, n)
                )
            if do_norm:
                norm_phase()
            elif do_feed:
                first_feed()
            elif do_attn:
                attn_loads()
                late_loads()
            copies.wait(*["l_" + n for n in links])
            if do_feed:
                if not do_norm:
                    copies.wait("r_st")
                feed_phase()
            if do_attn:
                if not do_feed:
                    product_starts()
                attn_phase()
            for n in loose:
                if n in ("dr1", "dr2"):
                    copies.start("o" + n, getattr(s, n), getattr(o, n))
            copies.wait_all()

        pl.when(i.section[0] == role)(run)
        if products:
            pl.when(i.section[0] != role)(product_starts)
            product_phase()

    local = {}
    if do_norm:
        names = ("head_weight", "weight_cot", "g2") if role == 1 else ("g2",)
        local.update({n: vectors[n] for n in names})
    if do_feed:
        local.update(g1=vectors["g1"])
    result = call(
        "backward_" + "_".join(phases), body, scalars, local, far, outs, scratch, 88,
        6_000_000_000 * len(phases), {n: made[n] for n in stacks} if made else None,
    )
    return dict(made or {}, **{n: result[n] for n in stacks}), {n: result[n] for n in loose}


def pick(array_in, index, axis):
    return lax.dynamic_index_in_dim(array_in, index, axis, keepdims=False)


def cut(array_in, start, size):
    return lax.dynamic_slice_in_dim(array_in, start, size, 0)


def added(*pieces):
    total = pieces[0].astype(F32)
    for piece in pieces[1:]:
        total = total + piece.astype(F32)
    return total


def routed(block, pairs):
    return lax.ppermute(block, "dp", pairs)


def swap_bit(block, bit):
    return routed(block, [(i, i ^ bit) for i in range(lax.axis_size("dp"))])


def behind(array_in, *others):
    return lax.optimization_barrier((array_in,) + others)[0]


def join(mine, got, start, cost):
    def kernel(start_ref, mine_ref, got_ref, sum_ref, send_ref):
        for j in range(4):
            sum_ref[j] = added(mine_ref[j], got_ref[j]).astype(BF)
        for j in range(3):
            send_ref[j] = sum_ref[start_ref[0] + j]

    local = pl.BlockSpec(memory_space=pltpu.VMEM)
    return pl.pallas_call(
        kernel,
        out_shape=[
            jax.ShapeDtypeStruct(mine.shape, BF),
            jax.ShapeDtypeStruct((3,) + mine.shape[1:], BF),
        ],
        in_specs=[pl.BlockSpec(memory_space=pltpu.SMEM), local, local],
        out_specs=[local, local],
        compiler_params=pltpu.CompilerParams(vmem_limit_bytes=32 << 20),
        cost_estimate=pl.CostEstimate(flops=cost, bytes_accessed=8_000_000, transcendentals=0),
        name="join_quarters",
    )(start, mine, got)


class ShardSum:
    def __init__(self, made):
        self.by_parts = "send" in made
        if not self.by_parts:
            self.grad = made["grad"]
            self.mark = (self.grad,)
            return
        me = lax.axis_index("dp")
        self.side, self.place = (me // 2) % 2, me // 4
        self.lower = self.place <= 1
        in_lines = lambda array: array.reshape((2, 4) + array.shape[1:])
        self.mine, self.got = in_lines(made["keep"]), swap_bit(in_lines(made["send"]), 1)
        self.mark = (made["send"],)

    def step(self, run, *before):
        if self.by_parts:
            if before:
                self.got = behind(self.got, *before)
            self.mark = (run(),)
        return self

    def to_line(self, *before):
        def run():
            mine, got, side = self.mine, self.got, self.side
            send = added(pick(mine, 1 - side, 0), pick(got, 1 - side, 0)).astype(BF)
            self.keep = added(pick(mine, side, 0), pick(got, side, 0)).astype(BF)
            self.got = swap_bit(send, 2)
            return send

        return self.step(run, *before)

    def inwards(self, *before, cost=1_000_000_000):
        def run():
            start = jnp.where(self.place == 0, 1, 0).astype(jnp.int32)[None]
            self.blocks, send = join(self.keep, self.got, start, cost)
            row = range(4)
            self.got = routed(send, [(j, j + 4) for j in row] + [(j + 12, j + 8) for j in row])
            return send

        return self.step(run, *before)

    def across(self, *before):
        def run():
            lower, row = self.lower, range(4)
            self.ends = self.got
            send = added(
                cut(self.blocks, jnp.where(lower, 2, 0), 2),
                cut(self.ends, jnp.where(lower, 1, 0), 2),
            ).astype(BF)
            self.got = routed(send, [(j + 4, j + 8) for j in row] + [(j + 8, j + 4) for j in row])
            return send

        return self.step(run, *before)

    def outwards(self, *before):
        def run():
            lower, row = self.lower, range(4)
            self.middle = self.got
            send = added(
                pick(self.blocks, jnp.where(lower, 0, 3), 0),
                pick(self.middle, jnp.where(lower, 0, 1), 0),
            ).astype(BF)
            self.got = routed(send, [(j + 4, j) for j in row] + [(j + 8, j + 12) for j in row])
            return send

        return self.step(run, *before)

    def last(self, *before):
        if not self.by_parts:
            return lax.psum_scatter(
                self.grad.astype(F32), "dp", scatter_dimension=0, tiled=True
            )
        got = behind(self.got, *before) if before else self.got
        total = added(
            pick(self.blocks, self.place, 0),
            pick(self.ends, jnp.where(self.lower, 0, 2), 0),
            pick(self.middle, jnp.where(self.lower, 1, 0), 0),
            got,
        )
        self.mark = (total,)
        return total


def body(
    tokens,
    out_cot,
    weight_cot,
    plan,
    lengths,
    q_weight,
    k_weight,
    v_weight,
    o_weight,
    q_bias,
    v_bias,
    o_bias,
    norm1_gain,
    norm1_bias,
    up_weight,
    up_bias,
    down_weight,
    down_bias,
    norm2_gain,
    norm2_bias,
    head_weight,
    head_bias,
):
    my_section = lax.axis_index("pipe")
    is_first = my_section == 0
    section = my_section.astype(jnp.int32)[None]
    row_count, half = tokens.shape
    wide, deep = up_weight.shape[1:]
    count = row_count // LONG
    dp_count = lax.axis_size("dp")
    share = wide // dp_count
    to_next, to_back = [(0, 1)], [(1, 0)]
    slab_of = lambda array, j: array[j * LONG : (j + 1) * LONG]
    over = lambda array, way: lax.ppermute(array, "pipe", way)
    token_other = [over(slab_of(tokens, 0), to_back)]
    for j in range(1, count):
        token_other.append(over(behind(slab_of(tokens, j), token_other[-1]), to_back))
    cot_other = over(out_cot, to_next)
    weights = dict(
        wq=q_weight, wk=k_weight, wv=v_weight, wo=o_weight, up=up_weight, down=down_weight
    )
    vectors = dict(
        qb=q_bias, vb=v_bias, ob=o_bias, g1=norm1_gain, b1=norm1_bias, upb=up_bias,
        downb=down_bias, g2=norm2_gain, b2=norm2_bias,
    )
    kept, recv = None, []
    for j in range(count):
        kept, sent = forward_slab(
            0, j, count, section, plan, lengths, tokens, token_other[j], None, weights, vectors,
            kept, [cot_other] if j else [],
        )
        recv.append(over(sent, to_next))
    mixed_got = []
    for j in range(count):
        kept, sent = forward_slab(
            1, j, count, section, plan, lengths, None, None, recv[j], weights, vectors, kept, []
        )
        mixed_got.append(over(sent, to_back))
    scalars = dict(section=section, plan=plan, lengths=lengths, head_bias=head_bias)
    vectors = dict(
        g1=norm1_gain, g2=norm2_gain, head_weight=head_weight[None],
        weight_cot=weight_cot.reshape(count, 1, LONG),
    )
    full = ("norm", "feed", "attn")
    made, recv = None, [None] * count
    for j in reversed(range(count)):
        made, loose = backward_slab(
            1, j, count, full, scalars, vectors, dict(own=out_cot, other=cot_other), weights, kept,
            {}, made, [mixed_got[count - 1 - j]],
        )
        recv[j] = over(loose["sent"], to_back)
    token_got = [None] * count
    for j in reversed(range(1, count)):
        made, loose = backward_slab(
            0, j, count, full, scalars, vectors, dict(recv=recv[j]), weights, kept, {}, made
        )
        token_got[j] = loose["sent"]
    head_sums = jnp.sum(made["vec0"][:, 3:5], axis=0)
    term = made["term"][:, 0].reshape(row_count)
    early = jnp.concatenate([term, head_sums[0], head_sums[1, :1]])
    scalars["core"] = (lax.axis_index("dp") % 2).astype(jnp.int32)[None]
    last = functools.partial(backward_slab, 0, 0, count)
    made, loose = last(
        ("norm",), scalars, vectors, dict(recv=recv[0]), weights, kept, {}, made, [],
        dp_count,
    )
    down_sum = ShardSum(loose).to_line()
    made, loose = last(
        ("feed",), scalars, vectors, {}, weights, kept, dict(loose, ddown=made["ddown"]), made,
        down_sum.mark, dp_count,
    )
    feed_sum = ShardSum(loose)
    down_sum.inwards(*feed_sum.mark, cost=60_000_000_000)
    feed_sum.to_line(*down_sum.mark)
    made, loose = last(
        ("attn",), scalars, vectors, {}, weights, kept, dict(loose, dbranch=made["dbranch"]), made,
        feed_sum.mark + down_sum.mark, dp_count,
    )
    qkv_sum = ShardSum(loose)
    down_sum.across(*qkv_sum.mark)
    feed_sum.inwards(*down_sum.mark, cost=60_000_000_000)
    qkv_sum.to_line(*feed_sum.mark)
    down_sum.outwards(*qkv_sum.mark)
    feed_sum.across(*down_sum.mark)
    early_got = over(behind(early, *down_sum.mark), to_back)
    token_got[0] = loose["sent"]
    token_got = [over(behind(array, *down_sum.mark), to_next) for array in token_got]
    qkv_sum.inwards(*feed_sum.mark, early_got)
    early = jnp.where(is_first, early_got, early)
    sums0, sums1, sums2 = (
        jnp.sum(behind(made[n], *qkv_sum.mark), axis=0) for n in ("vec0", "vec1", "vec2")
    )
    lines = jnp.concatenate(
        [sums2[:2], sums1[2:3], sums1[:2], sums0[2:3], sums0[:2], early[None, row_count:-1]]
    )
    flat = jnp.concatenate(
        [
            lines.reshape(9, dp_count, share).transpose(1, 0, 2).reshape(dp_count, -1),
            sums1[3 : 3 + deep // wide].reshape(dp_count, -1),
            jnp.broadcast_to(early[None, -1:], (dp_count, 1)),
        ],
        axis=1,
    )
    if qkv_sum.by_parts:
        flat = flat + swap_bit(flat, 1)
        flat = flat + swap_bit(flat, 2)
        qkv_sum.across(flat)
        feed_sum.outwards(*qkv_sum.mark)
        qkv_sum.outwards(*feed_sum.mark)
        flat = behind(flat, *qkv_sum.mark)
        near, far, farther = (swap_bit(flat, bits) for bits in (4, 8, 12))
        flat = pick((flat + near) + (far + farther), lax.axis_index("dp"), 0)
        down_grad = down_sum.last(*qkv_sum.mark)
        feed_grad = feed_sum.last(*qkv_sum.mark)
    else:
        flat = lax.psum_scatter(flat, "dp", scatter_dimension=0, tiled=True)[0]
        down_grad, feed_grad = down_sum.last(), feed_sum.last()
    qkv_grad = qkv_sum.last()
    up_grad, o_grad = feed_grad[:, :deep], feed_grad[:, deep:]
    at = lambda j: flat[j * share : (j + 1) * share]
    out_rows = kept["out"].reshape(row_count, wide)
    grad_rows = made["dh"].reshape(row_count, wide)
    others = jnp.concatenate(mixed_got), jnp.concatenate(token_got)
    others = [behind(array, flat) for array in others]
    mixed_out = jnp.where(is_first, others[0], out_rows[:, half:])
    tokens_grad = jnp.where(is_first, grad_rows[:, :half], others[1])
    return (
        mixed_out,
        early[:row_count],
        tokens_grad,
        qkv_grad[None, :, :wide],
        qkv_grad[None, :, wide : 2 * wide],
        qkv_grad[None, :, 2 * wide :],
        o_grad[None],
        at(0)[None],
        at(1)[None],
        at(2)[None],
        at(3)[None],
        at(4)[None],
        up_grad[None],
        flat[None, 9 * share : 9 * share + deep // dp_count],
        down_grad[None],
        at(5)[None],
        at(6)[None],
        at(7)[None],
        at(8),
        flat[-1:],
    )


def solution(mesh):
    rows, stack, flat = P("dp", "pipe"), P("pipe", None, None), P("pipe", None)
    in_specs = (
        (rows, rows, P("dp"), P("dp"), P("dp", None))
        + (stack,) * 4
        + (flat,) * 5
        + (stack, flat, stack, flat, flat, flat, P(), P())
    )
    shard, line = P("pipe", "dp", None), P("pipe", "dp")
    out_specs = (
        (rows, P("dp"), rows)
        + (shard,) * 4
        + (line,) * 5
        + (shard, line, shard, line, line, line, P("dp"), P())
    )
    return jax.shard_map(body, mesh=mesh, in_specs=in_specs, out_specs=out_specs, check_vma=False)
```
